128 devices in a mesh: nodes: 32 (over x, z, core), hid: 4 (over y).
Axes of the slice: x: 4, y: 4, z: 4, core: 2. Of those that a mesh axis runs over, the one named last changes fastest.
Arguments:
- features: bfloat16 [8192, 512], P('nodes', 'hid'), may hold values from -6 to 6
- neighbors: int32 [8192, 80], P('nodes'), may hold values from 0 to 767, as said below
- degree: int32 [8192], P('nodes'), may hold values from 1 to 80
- send_rows: int32 [32, 32, 16], P('nodes'), may hold values from 0 to 255, as said below
- node_count: int32 [32], P('nodes'), may hold values from 128 to 256, as said below
- w_first: bfloat16 [2, 512, 2048], P(None, None, 'hid'), may hold values from -0.1875 to 0.1875
- w_second: bfloat16 [2, 2048, 2048], P(None, 'hid'), may hold values from -0.09375 to 0.09375
- cotangent: bfloat16 [8192, 2048], P('nodes', 'hid'), may hold values from -6 to 6
Outputs:
- grad_w_first: float32 [512, 2, 2048], P('nodes', None, 'hid')
- grad_w_second: float32 [2048, 2, 2048], P('nodes', None, 'hid')
- grad_features: float32 [8192, 512], P('nodes', 'hid')
The draws below stay inside these ranges and needn't reach their ends.
Inputs may be any that keep to these rules, and one draw needn't show every extreme that they name: `neighbors`: for node i of partition q, each used entry is either a row below node_count[q] of q's own block or 256 + p * 16 + s naming slot s of what partition p != q sends to q; unused entries are 0. send_rows[p, q, s] is a row of partition p below node_count[p]. `node_count`: some partition is full in every draw.
All inputs are finite; a program needn't handle non-finite values.
Results may differ from the reference program's by a relative error of at most 0.024.
Values may be sent and summed in bfloat16 or wider, within the bound.
No kernel may reach another device: no remote copies, remote signals or barrier semaphores. Data moves between devices by JAX's collectives and lax.ppermute only.
A program may use at most 128 MiB of HBM per device.

```python
import jax
import jax.numpy as jnp
from jax import lax

D_IN = 512
HIDDEN_SIZE = 2048
K = 80
NODE_DEV = 256
HALO = 16
NODES = 8192
N_NODES = 32


def full_index(key):
    key = jax.random.fold_in(key, 101)
    return jax.random.randint(jax.random.fold_in(key, 1), (), 0, N_NODES).astype(jnp.int32)


def live_counts(key):
    full_part = full_index(key)
    key = jax.random.fold_in(key, 101)
    counts = jax.random.randint(key, (N_NODES,), NODE_DEV // 2, NODE_DEV + 1)
    return counts.at[full_part].set(NODE_DEV).astype(jnp.int32)


def degrees(key):
    key = jax.random.fold_in(key, 202)
    lower_pick = jax.random.randint(key, (N_NODES, NODE_DEV), 1, K + 1)
    upper_pick = jax.random.randint(jax.random.fold_in(key, 1), (N_NODES, NODE_DEV), 1, K + 1)
    degree_table = jnp.minimum(lower_pick, upper_pick)
    degree_table = degree_table.at[:, 0].set(K).at[:, 1].set(1)
    return degree_table.reshape(N_NODES * NODE_DEV).astype(jnp.int32)


def draw_node_count(key, part):
    return live_counts(key)


def draw_degree(key, part):
    return degrees(key)


def draw_send_rows(key, part):
    counts = live_counts(key)
    full_part = full_index(key)
    key = jax.random.fold_in(key, 3)
    table = jax.random.randint(key, (N_NODES, N_NODES, HALO), 0, counts[:, None, None])
    target = (full_part + 1) % N_NODES
    table = table.at[full_part, target, 0].set(NODE_DEV - 1).at[full_part, target, 1].set(0)
    return table.astype(jnp.int32)


def draw_neighbors(key, part):
    counts = live_counts(key)
    degree_table = degrees(key).reshape(N_NODES, NODE_DEV)
    key = jax.random.fold_in(key, 4)
    shape = (N_NODES, NODE_DEV, K)
    own_slot = jax.random.randint(jax.random.fold_in(key, 1), shape, 0, counts[:, None, None])
    hop_count = jax.random.randint(jax.random.fold_in(key, 2), shape, 0, N_NODES - 1)
    own_part = jnp.arange(N_NODES, dtype=jnp.int32)[:, None, None]
    peer_part = (own_part + 1 + hop_count) % N_NODES
    slot_pick = jax.random.randint(jax.random.fold_in(key, 3), shape, 0, HALO)
    far_slot = NODE_DEV + peer_part * HALO + slot_pick
    remote_pick = jax.random.randint(jax.random.fold_in(key, 4), shape, 0, 2)
    chosen = jnp.where(remote_pick == 1, far_slot, own_slot)
    position = jnp.arange(K, dtype=jnp.int32)[None, None, :]
    chosen = jnp.where(position < degree_table[:, :, None], chosen, 0)
    chosen = chosen.at[0, 0, 0].set(NODE_DEV + N_NODES * HALO - 1)
    return chosen.reshape(N_NODES * NODE_DEV, K).astype(jnp.int32)


def raised(array, key, source, target, parts, factor):
    owner, partner = [(jnp.arange(array.shape[dim]) // (array.shape[dim] // parts)).reshape([-1 if axis == dim else 1 for axis in range(array.ndim)]) for dim in (source, target)]
    chosen = jax.random.permutation(key, parts)[partner]
    strong = (owner == chosen) | (owner == (partner + parts // 2) % parts)
    return jnp.where(strong, factor * array, array)


def steps_of(stream_key, shape, shards, smallest, top_value):
    gain, own = 1.0, jax.random.fold_in(stream_key, 6)
    for dim, parts in shards:
        steps = jnp.exp(jax.random.uniform(jax.random.fold_in(own, dim), (parts,), jnp.float32, smallest / len(shards), top_value / len(shards)))
        gain = gain * jnp.repeat(steps, shape[dim] // parts).reshape([-1 if axis == dim else 1 for axis in range(len(shape))])
    return gain


def centred(stream_key, dims, width, reach, pieces=(), held_as=jnp.bfloat16):
    level = steps_of(stream_key, dims, pieces, -0.22, 0.18) if pieces else 1.0
    result = jax.random.normal(stream_key, dims, jnp.float32) * width * level
    return jnp.minimum(jnp.maximum(result, -reach), reach).astype(held_as)


def gaussian_with(own_key, extent, scale, most, cuts, heavy, kind=jnp.bfloat16):
    array = scale * jax.random.normal(own_key, extent, jnp.float32)
    if cuts:
        array = array * steps_of(own_key, extent, cuts, -0.22, 0.18)
    return jnp.clip(raised(array, jax.random.fold_in(own_key, 3), *heavy), -most, most).astype(kind)


def setup_inputs(seed: int = 0) -> dict:
    keys = jax.random.split(jax.random.key(seed), 9)
    return {
        "features": gaussian_with(keys[0], (NODES, D_IN), 1.0, 6.0, ((0, 32), (1, 4)), (0, 1, 32, 2.75)),
        "neighbors": draw_neighbors(jax.random.fold_in(keys[8], 71), 0),
        "degree": draw_degree(jax.random.fold_in(keys[8], 71), 0),
        "send_rows": draw_send_rows(jax.random.fold_in(keys[8], 71), 0),
        "node_count": draw_node_count(jax.random.fold_in(keys[8], 71), 0),
        "w_first": centred(keys[5], (2, D_IN, HIDDEN_SIZE), (2 * D_IN) ** -0.5, 0.1875, ((2, 4),)),
        "w_second": centred(keys[6], (2, HIDDEN_SIZE, HIDDEN_SIZE), (2 * HIDDEN_SIZE) ** -0.5, 0.09375, ((1, 4),)),
        "cotangent": gaussian_with(keys[7], (NODES, HIDDEN_SIZE), 1.0, 6.0, ((0, 32), (1, 4)), (0, 1, 32, 2.75)),
    }


def silu_slope(value):
    sig = jax.nn.sigmoid(value)
    return sig * (1.0 + value * (1.0 - sig))


def sources(neighbors, degree, send_rows):
    total = NODE_DEV * N_NODES
    partition = (jnp.arange(total, dtype=jnp.int32) // NODE_DEV)[:, None]
    own_index = partition * NODE_DEV + neighbors
    offset = jnp.maximum(neighbors - NODE_DEV, 0)
    peer_index = jnp.minimum(offset // HALO, N_NODES - 1).astype(jnp.int32)
    slot_index = (offset % HALO).astype(jnp.int32)
    far_index = peer_index * NODE_DEV + send_rows[peer_index, partition, slot_index]
    source = jnp.where(neighbors < NODE_DEV, own_index, far_index).astype(jnp.int32)
    slot_used = jnp.arange(K, dtype=jnp.int32)[None, :] < degree[:, None]
    return source, slot_used


def aggregate(values, source, slot_used, divisor):
    def add_one(totals, position):
        target = jnp.take(source, position, axis=1)
        picked = jnp.take(values, target, axis=0).astype(jnp.float32)
        keep = jnp.take(slot_used, position, axis=1)[:, None]
        return totals + jnp.where(keep, picked, jnp.zeros_like(picked)), None

    start_sum = jnp.zeros((values.shape[0], values.shape[1]), jnp.float32)
    totals, unused = lax.scan(add_one, start_sum, jnp.arange(K, dtype=jnp.int32))
    return totals / divisor


def spread(grads, source, slot_used):
    terms = grads.astype(jnp.float32)

    def add_one(totals, position):
        target = jnp.take(source, position, axis=1)
        keep = jnp.take(slot_used, position, axis=1)[:, None]
        return totals.at[target].add(jnp.where(keep, terms, jnp.zeros_like(terms))), None

    start_sum = jnp.zeros((grads.shape[0], grads.shape[1]), jnp.float32)
    totals, unused = lax.scan(add_one, start_sum, jnp.arange(K, dtype=jnp.int32))
    return totals


def reference(features, neighbors, degree, send_rows, node_count, w_first, w_second, cotangent):
    total = NODE_DEV * N_NODES
    source, slot_used = sources(neighbors, degree, send_rows)
    divisor = degree.astype(jnp.float32)[:, None]
    index = jnp.arange(total, dtype=jnp.int32)
    live_rows = ((index % NODE_DEV) < node_count[index // NODE_DEV])[:, None]
    grad_scale = float(total) ** -0.5
    agg_features = aggregate(features, source, slot_used, divisor).astype(jnp.bfloat16)
    pre_first = jnp.dot(features, w_first[0], preferred_element_type=jnp.float32) + jnp.dot(agg_features, w_first[1], preferred_element_type=jnp.float32)
    hidden_one = jax.nn.silu(pre_first).astype(jnp.bfloat16)
    agg_hidden = aggregate(hidden_one, source, slot_used, divisor).astype(jnp.bfloat16)
    pre_second = jnp.dot(hidden_one, w_second[0], preferred_element_type=jnp.float32) + jnp.dot(agg_hidden, w_second[1], preferred_element_type=jnp.float32)
    slope_two = cotangent.astype(jnp.float32) * silu_slope(pre_second)
    grad_second = jnp.where(live_rows, slope_two, jnp.zeros_like(slope_two)).astype(jnp.bfloat16)
    grad_w_second = jnp.stack([jnp.dot(grad_second.T, hidden_one, preferred_element_type=jnp.float32), jnp.dot(grad_second.T, agg_hidden, preferred_element_type=jnp.float32)], axis=1) * grad_scale
    grad_agg_hidden = (jnp.dot(grad_second, w_second[1].T, preferred_element_type=jnp.float32) / divisor).astype(jnp.bfloat16)
    grad_hidden = jnp.dot(grad_second, w_second[0].T, preferred_element_type=jnp.float32) + spread(grad_agg_hidden, source, slot_used)
    grad_first = (grad_hidden * silu_slope(pre_first)).astype(jnp.bfloat16)
    grad_w_first = jnp.stack([jnp.dot(features.T, grad_first, preferred_element_type=jnp.float32), jnp.dot(agg_features.T, grad_first, preferred_element_type=jnp.float32)], axis=1) * grad_scale
    grad_agg_features = (jnp.dot(grad_first, w_first[1].T, preferred_element_type=jnp.float32) / divisor).astype(jnp.bfloat16)
    grad_features = jnp.dot(grad_first, w_first[0].T, preferred_element_type=jnp.float32) + spread(grad_agg_features, source, slot_used)
    return grad_w_first, grad_w_second, grad_features
```

```python
import jax
import jax.numpy as jnp
from jax import lax
from jax.experimental import pallas as pl
from jax.experimental.pallas import tpu as pltpu
from jax.sharding import PartitionSpec as P

BF16 = jnp.bfloat16
F32 = jnp.float32
ROWS = 256
PEERS = 32
SLOTS = 16
FAR = PEERS * SLOTS
HID = 4
LANES = 128
UNITS = 512
KEPT = 80


def mm(left_op, right_op):
    return jnp.dot(left_op, right_op, preferred_element_type=F32)


def mm_last(left_op, right_op):
    return lax.dot_general(left_op, right_op, (((1,), (1,)), ((), ())), preferred_element_type=F32)


def mm_first(left_op, right_op):
    return lax.dot_general(left_op, right_op, (((0,), (0,)), ((), ())), preferred_element_type=F32)


def wide(column, width):
    return jnp.concatenate([column] * (width // LANES), axis=1)


def pick_kernel(routes_ref, feat_ref, sel_ref, selt_ref, send_ref):
    row = lax.broadcasted_iota(jnp.int32, (ROWS, FAR), 0)
    chosen = jnp.where(row == routes_ref[...], 1.0, 0.0)
    selt_ref[...] = chosen.astype(BF16)
    sel = chosen.T.astype(BF16)
    sel_ref[...] = sel
    picked = mm(sel, feat_ref[...]).astype(BF16).reshape(PEERS, SLOTS, LANES)
    for part in range(HID):
        send_ref[:, part] = picked


def count_kernel(neigh_ref, degree_ref, adj_ref, adjt_ref, inv_ref, deg_ref):
    deg_ref[...] = jnp.broadcast_to(degree_ref[...].astype(F32), (LANES, ROWS)).T
    inv_ref[...] = 1.0 / deg_ref[...]
    group = 32

    def step(index, carry):
        rows = pl.ds(pl.multiple_of(index * group, group), group)
        entry = neigh_ref[rows, :]
        place = lax.broadcasted_iota(jnp.int32, (group, KEPT), 1).astype(F32)
        used = place < deg_ref[rows, :][:, :KEPT]
        block = entry >> 7
        upper = block >= 3
        key = (entry & 127) + jnp.where(upper, LANES, 0)
        weight = jnp.where(used, jnp.left_shift(1, 10 * jnp.where(upper, block - 3, block)), 0)
        lane = lax.broadcasted_iota(jnp.int32, (group, LANES), 1)
        low = jnp.zeros((group, LANES), jnp.int32)
        high = jnp.zeros((group, LANES), jnp.int32)
        for j in range(KEPT):
            key_j = jnp.broadcast_to(key[:, j : j + 1], (group, LANES))
            weight_j = jnp.broadcast_to(weight[:, j : j + 1], (group, LANES))
            low = low + jnp.where(key_j == lane, weight_j, 0)
            high = high + jnp.where(key_j == lane + LANES, weight_j, 0)
        for t in range(3):
            for base, packed in ((0, low), (3, high)):
                count = jnp.right_shift(packed, 10 * t) & 1023
                adj_ref[rows, (base + t) * LANES : (base + t + 1) * LANES] = count.astype(F32).astype(BF16)
        return carry

    lax.fori_loop(0, ROWS // group, step, 0)
    for t in range((ROWS + FAR) // LANES):
        cols = slice(t * LANES, (t + 1) * LANES)
        adjt_ref[cols, :] = adj_ref[:, cols].astype(F32).T.astype(BF16)


def first_kernel(
    place_ref, f0, f1, f2, f3, far_ref, adj_ref, inv_ref, w_ref, sel_ref,
    both_ref, hidden_ref, slope_ref, send_ref, ext_ref,
):
    me = place_ref[0]
    for d, piece in enumerate((f0, f1, f2, f3)):
        origin = lax.rem(me + HID - d, HID)
        cols = pl.ds(pl.multiple_of(origin * LANES, LANES), LANES)
        ext_ref[:ROWS, cols] = piece[...]
    for origin in range(HID):
        ext_ref[ROWS:, origin * LANES : (origin + 1) * LANES] = far_ref[:, origin].reshape(FAR, LANES)
    both_ref[:, :UNITS] = ext_ref[:ROWS, :]
    agg = mm(adj_ref[...], ext_ref[...]) * wide(inv_ref[...], UNITS)
    both_ref[:, UNITS:] = agg.astype(BF16)
    pre = mm(both_ref[...], w_ref[...])
    sig = 1.0 / (1.0 + jnp.exp(-pre))
    hidden = (pre * sig).astype(BF16)
    hidden_ref[...] = hidden
    slope_ref[...] = sig * (1.0 + pre * (1.0 - sig))
    send_ref[...] = mm(sel_ref[...], hidden).astype(BF16).reshape(PEERS, SLOTS, UNITS)


def second_kernel(
    place_ref, hidden_ref, far_ref, adj_ref, inv_ref, w_ref, stacked_ref, own_ref, s1, s2, s3
):
    me = place_ref[0]
    hidden = hidden_ref[...]
    total = mm(adj_ref[:, :ROWS], hidden) + mm(adj_ref[:, ROWS:], far_ref[...].reshape(FAR, UNITS))
    stacked_ref[:, :UNITS] = hidden
    stacked_ref[:, UNITS:] = (total * wide(inv_ref[...], UNITS)).astype(BF16)
    for d, out in ((2, s2), (1, s1), (3, s3), (0, own_ref)):
        target = lax.rem(me + d, HID)
        cols = pl.ds(pl.multiple_of(target * UNITS, UNITS), UNITS)
        out[...] = mm(stacked_ref[...], w_ref[:, cols]).astype(out.dtype)


def slope_kernel(place_ref, own_ref, r1, r2, r3, cot_ref, grad_ref):
    pre = own_ref[...] + r1[...].astype(F32) + r2[...].astype(F32) + r3[...].astype(F32)
    sig = 1.0 / (1.0 + jnp.exp(-pre))
    slope = cot_ref[...].astype(F32) * (sig * (1.0 + pre * (1.0 - sig)))
    live = lax.broadcasted_iota(jnp.int32, (ROWS, UNITS), 0) < place_ref[2]
    grad_ref[...] = jnp.where(live, slope, 0.0).astype(BF16)


def spread_kernel(place_ref, g0, g1, g2, g3, w_ref, inv_ref, adjt_ref, mean_ref, halo_ref):
    me = place_ref[0]
    total = jnp.zeros((ROWS, UNITS), F32)
    for d, grad in enumerate((g0, g1, g2, g3)):
        origin = lax.rem(me + HID - d, HID)
        cols = pl.ds(pl.multiple_of(origin * UNITS, UNITS), UNITS)
        total = total + mm_last(grad[...], w_ref[UNITS:, cols])
    mean = (total * wide(inv_ref[...], UNITS)).astype(BF16)
    mean_ref[...] = mean
    halo_ref[...] = mm(adjt_ref[ROWS:, :], mean).astype(BF16).reshape(PEERS, SLOTS, UNITS)


def own_kernel(place_ref, g0, g1, g2, g3, w_ref, mean_ref, adjt_ref, own_ref):
    me = place_ref[0]
    total = mm(adjt_ref[:ROWS, :], mean_ref[...])
    for d, grad in enumerate((g0, g1, g2, g3)):
        origin = lax.rem(me + HID - d, HID)
        cols = pl.ds(pl.multiple_of(origin * UNITS, UNITS), UNITS)
        total = total + mm_last(grad[...], w_ref[:UNITS, cols])
    own_ref[...] = total


def outer_second_kernel(scale, place_ref, g0, g1, g2, g3, stacked_ref, keep_ref, give_ref):
    me = place_ref[0]
    core = place_ref[1]
    for d, grad in enumerate((g0, g1, g2, g3)):
        origin = lax.rem(me + HID - d, HID)
        blocks = pl.ds(origin * HID, HID)
        product = (mm_first(grad[...], stacked_ref[...]) * scale).astype(BF16)
        product = product.reshape(HID, 2, 64, 2 * UNITS)

        @pl.when(core == 0)
        def _():
            keep_ref[blocks] = product[:, 0]
            give_ref[blocks] = product[:, 1]

        @pl.when(core == 1)
        def _():
            keep_ref[blocks] = product[:, 1]
            give_ref[blocks] = product[:, 0]


def add_kernel(left_ref, right_ref, out_ref):
    out_ref[...] = (left_ref[...].astype(F32) + right_ref[...].astype(F32)).astype(BF16)


def settle_kernel(
    back_ref, own_ref, slope_ref, selt_ref, w_ref, inv_ref, adjt_ref, grad_ref, mean_ref, halo_ref
):
    grad = own_ref[...] + mm(selt_ref[...], back_ref[...].reshape(FAR, UNITS))
    grad = (grad * slope_ref[...]).astype(BF16)
    grad_ref[...] = grad
    mean = (mm_last(grad, w_ref[UNITS:, :]) * wide(inv_ref[...], UNITS)).astype(BF16)
    mean_ref[...] = mean
    halo = mm(adjt_ref[ROWS:, :], mean).astype(BF16)
    for part in range(HID):
        halo_ref[:, part] = halo[:, part * LANES : (part + 1) * LANES].reshape(PEERS, SLOTS, LANES)


def share_kernel(place_ref, grad_ref, mean_ref, w_ref, adjt_ref, own_ref, s1, s2, s3, total_ref):
    me = place_ref[0]
    total_ref[...] = mm_last(grad_ref[...], w_ref[:UNITS, :]) + mm(adjt_ref[:ROWS, :], mean_ref[...])
    for d, out in ((2, s2), (1, s1), (3, s3), (0, own_ref)):
        target = lax.rem(me + d, HID)
        cols = pl.ds(pl.multiple_of(target * LANES, LANES), LANES)
        out[...] = total_ref[:, cols].astype(out.dtype)


def outer_first_kernel(scale, both_ref, grad_ref, out_ref):
    product = (mm_first(both_ref[...], grad_ref[...]) * scale).astype(BF16)
    product = product.reshape(2, PEERS, SLOTS, UNITS)
    out_ref[:, :SLOTS] = product[0]
    out_ref[:, SLOTS:] = product[1]


def final_kernel(own_ref, r1, r2, r3, selt_ref, back_ref, out_ref):
    total = own_ref[...] + r1[...].astype(F32) + r2[...].astype(F32) + r3[...].astype(F32)
    for origin in range(HID):
        total = total + mm(selt_ref[...], back_ref[:, origin].reshape(FAR, LANES))
    out_ref[...] = total


def sum_kernel(parts_ref, out_ref):
    total = parts_ref[0].astype(F32)
    for index in range(1, parts_ref.shape[0]):
        total = total + parts_ref[index].astype(F32)
    out_ref[...] = total


def call(kernel, name, operands, outs, scratch=(), flops=0, scalars=0):
    shapes = [jax.ShapeDtypeStruct(shape, dtype) for shape, dtype in outs]
    in_specs = [
        pl.BlockSpec(memory_space=pltpu.SMEM if index < scalars else pltpu.VMEM)
        for index in range(len(operands))
    ]
    moved = sum(o.size * o.dtype.itemsize for o in list(operands) + shapes)
    results = pl.pallas_call(
        kernel,
        out_shape=shapes,
        in_specs=in_specs,
        out_specs=[pl.BlockSpec(memory_space=pltpu.VMEM) for _ in shapes],
        scratch_shapes=list(scratch),
        compiler_params=pltpu.CompilerParams(vmem_limit_bytes=32 * 1024 * 1024),
        cost_estimate=pl.CostEstimate(flops=flops, bytes_accessed=moved, transcendentals=0),
        name=name,
    )(*operands)
    return results[0] if len(outs) == 1 else results


def around(values):
    return [lax.ppermute(v, "hid", [(i, (i + d) % HID) for i in range(HID)]) for d, v in values]


def on_device(features, neighbors, degree, send_rows, node_count, w_first, w_second, cotangent):
    hid = lax.axis_index("hid").astype(jnp.int32)
    node = lax.axis_index("nodes").astype(jnp.int32)
    place = jnp.stack([hid, node % 2, node_count[0]])
    scale = float(ROWS * PEERS) ** (-0.5)
    routes = send_rows.reshape(1, FAR)
    w1 = w_first.reshape(2 * UNITS, UNITS)
    w2 = w_second.reshape(2 * UNITS, HID * UNITS)
    big = 2 * ROWS * UNITS * UNITS

    sel, selt, send_feat = call(
        pick_kernel, "pick", (routes, features),
        [((FAR, ROWS), BF16), ((ROWS, FAR), BF16), ((PEERS, HID, SLOTS, LANES), BF16)],
        flops=2 * FAR * ROWS * LANES,
    )
    far_feat = lax.all_to_all(
        send_feat.reshape(PEERS * HID, SLOTS, LANES), ("nodes", "hid"), 0, 0, tiled=True
    ).reshape(PEERS, HID, SLOTS, LANES)
    f1, f2, f3 = around([(1, features), (2, features), (3, features)])
    adj, adjt, inv = call(
        count_kernel, "count", (neighbors, degree.reshape(1, ROWS)),
        [((ROWS, ROWS + FAR), BF16), ((ROWS + FAR, ROWS), BF16), ((ROWS, LANES), F32)],
        scratch=[pltpu.VMEM((ROWS, LANES), F32)],
        flops=4 * big,
    )
    both, hidden, slope, send_hidden = call(
        first_kernel, "first",
        (place, features, f1, f2, f3, far_feat, adj, inv, w1, sel),
        [
            ((ROWS, 2 * UNITS), BF16), ((ROWS, UNITS), BF16), ((ROWS, UNITS), F32),
            ((PEERS, SLOTS, UNITS), BF16),
        ],
        scratch=[pltpu.VMEM((ROWS + FAR, UNITS), BF16)],
        flops=8 * big, scalars=1,
    )
    far_hidden = lax.all_to_all(send_hidden, "nodes", 0, 0, tiled=True)
    stacked, own_pre, s1, s2, s3 = call(
        second_kernel, "second",
        (place, hidden, far_hidden, adj, inv, w2),
        [((ROWS, 2 * UNITS), BF16), ((ROWS, UNITS), F32)] + [((ROWS, UNITS), BF16)] * 3,
        flops=10 * big, scalars=1,
    )
    r2, r1, r3 = around([(2, s2), (1, s1), (3, s3)])
    g0 = call(
        slope_kernel, "slope", (place, own_pre, r1, r2, r3, cotangent),
        [((ROWS, UNITS), BF16)], scalars=1,
    )
    g2, g1, g3 = around([(2, g0), (1, g0), (3, g0)])
    mean_hidden, halo_hidden = call(
        spread_kernel, "spread", (place, g0, g1, g2, g3, w2, inv, adjt),
        [((ROWS, UNITS), BF16), ((PEERS, SLOTS, UNITS), BF16)],
        flops=5 * big, scalars=1,
    )
    back_hidden = lax.all_to_all(halo_hidden, "nodes", 0, 0, tiled=True)
    own_hidden = call(
        own_kernel, "own", (place, g0, g1, g2, g3, w2, mean_hidden, adjt),
        [((ROWS, UNITS), F32)], flops=5 * big, scalars=1,
    )
    keep, give = call(
        lambda *refs: outer_second_kernel(scale, *refs), "outer_second",
        (place, g0, g1, g2, g3, stacked),
        [((16, 64, 2 * UNITS), BF16)] * 2,
        flops=8 * big, scalars=1,
    )
    got = lax.ppermute(give, "nodes", [(i, i ^ 1) for i in range(PEERS)])
    pair = call(add_kernel, "pair", (keep, got), [((16, 64, 2 * UNITS), BF16)])
    grad, mean_first, halo_first = call(
        settle_kernel, "settle",
        (back_hidden, own_hidden, slope, selt, w1, inv, adjt),
        [((ROWS, UNITS), BF16), ((ROWS, UNITS), BF16), ((PEERS, HID, SLOTS, LANES), BF16)],
        flops=4 * big,
    )
    back_first = lax.all_to_all(
        halo_first.reshape(PEERS * HID, SLOTS, LANES), ("nodes", "hid"), 0, 0, tiled=True
    ).reshape(PEERS, HID, SLOTS, LANES)
    outer_first = call(
        lambda *refs: outer_first_kernel(scale, *refs), "outer_first", (both, grad),
        [((PEERS, 2 * SLOTS, UNITS), BF16)], flops=2 * big,
    )
    parts_first = lax.all_to_all(outer_first, "nodes", 0, 0, tiled=True)
    own_share, t1, t2, t3 = call(
        share_kernel, "share", (place, grad, mean_first, w1, adjt),
        [((ROWS, LANES), F32)] + [((ROWS, LANES), BF16)] * 3,
        scratch=[pltpu.VMEM((ROWS, UNITS), F32)],
        flops=2 * big, scalars=1,
    )
    u2, u1, u3 = around([(2, t2), (1, t1), (3, t3)])
    same_core = [[2 * chip + core for chip in range(16)] for core in range(2)]
    parts_second = lax.all_to_all(pair, "nodes", 0, 0, tiled=True, axis_index_groups=same_core)
    grad_w_second = call(sum_kernel, "sum_second", (parts_second,), [((64, 2 * UNITS), F32)])
    grad_features = call(
        final_kernel, "final", (own_share, u1, u2, u3, selt, back_first),
        [((ROWS, LANES), F32)], flops=big,
    )
    grad_w_first = call(sum_kernel, "sum_first", (parts_first,), [((2 * SLOTS, UNITS), F32)])
    return (
        jnp.swapaxes(grad_w_first.reshape(2, SLOTS, UNITS), 0, 1),
        grad_w_second.reshape(64, 2, UNITS),
        grad_features,
    )


def solution(mesh):
    placed = (
        P("nodes", "hid"),
        P("nodes", None),
        P("nodes"),
        P("nodes", None, None),
        P("nodes"),
        P(None, None, "hid"),
        P(None, "hid", None),
        P("nodes", "hid"),
    )
    return jax.shard_map(
        on_device,
        mesh=mesh,
        in_specs=placed,
        out_specs=(P("nodes", None, "hid"), P("nodes", None, "hid"), P("nodes", "hid")),
        check_vma=False,
    )
```

```python
import math

import jax
import jax.numpy as jnp
from jax import lax
from jax.experimental import pallas as pl
from jax.experimental.pallas import tpu as pltpu
from jax.sharding import PartitionSpec as P

BF16 = jnp.bfloat16
F32 = jnp.float32
ROWS = 256
PEERS = 32
SLOTS = 16
FAR = PEERS * SLOTS
HID = 4
LANES = 128
UNITS = 512
KEPT = 80
BIG = 2 * ROWS * UNITS * UNITS


def mm(left_op, right_op):
    return jnp.dot(left_op, right_op, preferred_element_type=F32)


def mm_last(left_op, right_op):
    return lax.dot_general(left_op, right_op, (((1,), (1,)), ((), ())), preferred_element_type=F32)


def mm_first(left_op, right_op):
    return lax.dot_general(left_op, right_op, (((0,), (0,)), ((), ())), preferred_element_type=F32)


def wide(column, width):
    return jnp.concatenate([column] * (width // LANES), axis=1)


def route_rows(routes_ref):
    peer = lax.broadcasted_iota(jnp.int32, (PEERS, FAR), 0)
    lane_peer = lax.broadcasted_iota(jnp.int32, (PEERS, FAR), 1) >> 4
    spread_out = jnp.where(peer == lane_peer, 1.0, 0.0).astype(BF16)
    by_slot = mm(routes_ref[...].astype(F32).astype(BF16), spread_out)
    slot = lax.broadcasted_iota(jnp.int32, (SLOTS, FAR), 0)
    lane_slot = lax.broadcasted_iota(jnp.int32, (SLOTS, FAR), 1) & (SLOTS - 1)
    routes = jnp.sum(jnp.where(slot == lane_slot, by_slot, 0.0), axis=0, keepdims=True)
    row = lax.broadcasted_iota(jnp.int32, (ROWS, FAR), 0).astype(F32)
    return jnp.where(row == routes, 1.0, 0.0)


def pick_kernel(place, f0, f1, f2, f3, sel_ref, full_ref, send_ref):
    for d, piece in enumerate((f0, f1, f2, f3)):
        origin = lax.rem(place.hid + HID - d, HID)
        full_ref[:, pl.ds(pl.multiple_of(origin * LANES, LANES), LANES)] = piece[...]
    send_ref[...] = mm(sel_ref[...], full_ref[...]).astype(BF16).reshape(PEERS, SLOTS, UNITS)


def count_kernel(
    neigh_ref, degree_ref, routes_ref, adj_ref, adjt_ref, inv_ref, sel_ref, selt_ref, key_ref, low_ref, high_ref
):
    chosen = route_rows(routes_ref)
    selt_ref[...] = chosen.astype(BF16)
    sel_ref[...] = chosen.T.astype(BF16)
    inv_ref[...] = 1.0 / jnp.broadcast_to(degree_ref[...].astype(F32), (LANES, ROWS)).T
    entry = neigh_ref[...]
    used = lax.broadcasted_iota(jnp.int32, (KEPT, ROWS), 0) < degree_ref[...]
    block = entry >> 7
    upper = block >= 3
    weight = jnp.where(used, jnp.left_shift(1, 10 * jnp.where(upper, block - 3, block)), 0)
    key_ref[...] = entry & (LANES - 1)
    low_ref[...] = jnp.where(upper, 0, weight)
    high_ref[...] = jnp.where(upper, weight, 0)
    tall = 64
    for half in range(LANES // tall):
        value = lax.broadcasted_iota(jnp.int32, (tall, LANES), 0) + half * tall
        for side in range(ROWS // LANES):
            cols = slice(side * LANES, (side + 1) * LANES)

            def step(index, carry):
                low, high = carry
                at = pl.ds(pl.multiple_of(index * 8, 8), 8)
                keys, lows, highs = key_ref[at, cols], low_ref[at, cols], high_ref[at, cols]
                for j in range(8):
                    same = keys[j : j + 1] == value
                    low = low + jnp.where(same, lows[j : j + 1], 0)
                    high = high + jnp.where(same, highs[j : j + 1], 0)
                return low, high

            empty = jnp.zeros((tall, LANES), jnp.int32)
            low, high = lax.fori_loop(0, KEPT // 8, step, (empty, empty))
            for t in range(3):
                for base, packed in ((0, low), (3, high)):
                    count = jnp.right_shift(packed, 10 * t) & 1023
                    start = (base + t) * LANES + half * tall
                    adjt_ref[start : start + tall, cols] = count.astype(F32).astype(BF16)
    for t in range((ROWS + FAR) // LANES):
        rows = slice(t * LANES, (t + 1) * LANES)
        adj_ref[:, rows] = adjt_ref[rows, :].astype(F32).T.astype(BF16)


def first_kernel(full_ref, far_ref, adj_ref, inv_ref, w_ref, sel_ref, both_ref, hidden_ref, send_ref):
    full = full_ref[...]
    agg = mm(adj_ref[:, :ROWS], full) + mm(adj_ref[:, ROWS:], far_ref[...].reshape(FAR, UNITS))
    both_ref[:, :UNITS] = full
    both_ref[:, UNITS:] = (agg * wide(inv_ref[...], UNITS)).astype(BF16)
    pre = mm(both_ref[...], w_ref[...])
    sig = 1.0 / (1.0 + jnp.exp(-pre))
    hidden = (pre * sig).astype(BF16)
    hidden_ref[...] = hidden
    send_ref[...] = mm(sel_ref[...], hidden).astype(BF16).reshape(PEERS, SLOTS, UNITS)


def gate_kernel(both_ref, stacked_ref, w1_ref, slope_ref, saved_ref):
    saved_ref[...] = stacked_ref[...]
    pre = mm(both_ref[...], w1_ref[...])
    sig = 1.0 / (1.0 + jnp.exp(-pre))
    slope_ref[...] = sig * (1.0 + pre * (1.0 - sig))


def second_kernel(
    place, hidden_ref, far_ref, adj_ref, inv_ref, w_ref, stacked_ref, own_ref, s1, s2, s3
):
    hidden = hidden_ref[...]
    total = mm(adj_ref[:, :ROWS], hidden) + mm(adj_ref[:, ROWS:], far_ref[...].reshape(FAR, UNITS))
    stacked_ref[:, :UNITS] = hidden
    stacked_ref[:, UNITS:] = (total * wide(inv_ref[...], UNITS)).astype(BF16)
    for d, out in ((2, s2), (1, s1), (3, s3), (0, own_ref)):
        target = lax.rem(place.hid + d, HID)
        cols = pl.ds(pl.multiple_of(target * UNITS, UNITS), UNITS)
        out[...] = mm(stacked_ref[...], w_ref[:, cols]).astype(out.dtype)


def slope_kernel(count_ref, own_ref, r1, r2, r3, cot_ref, grad_ref):
    pre = own_ref[...] + r1[...].astype(F32) + r2[...].astype(F32) + r3[...].astype(F32)
    sig = 1.0 / (1.0 + jnp.exp(-pre))
    slope = cot_ref[...].astype(F32) * (sig * (1.0 + pre * (1.0 - sig)))
    live = lax.broadcasted_iota(jnp.int32, (ROWS, UNITS), 0) < count_ref[0]
    grad_ref[...] = jnp.where(live, slope, 0.0).astype(BF16)


def spread_kernel(place, g0, g1, g2, g3, w_ref, inv_ref, adjt_ref, halo_ref, own_ref, others_ref):
    order = ((0, g0), (3, g3), (1, g1), (2, g2))
    for index, grad in enumerate((g1, g2, g3)):
        others_ref[index] = grad[...]

    def back(base):
        total = None
        for d, grad in order:
            origin = lax.rem(place.hid + HID - d, HID)
            cols = pl.ds(pl.multiple_of(origin * UNITS, UNITS), UNITS)
            term = mm_last(grad[...], w_ref[base : base + UNITS, cols])
            total = term if total is None else total + term
        return total

    mean = (back(UNITS) * wide(inv_ref[...], UNITS)).astype(BF16)
    halo_ref[...] = mm(adjt_ref[ROWS:, :], mean).astype(BF16).reshape(PEERS, SLOTS, UNITS)
    own_ref[...] = back(0) + mm(adjt_ref[:ROWS, :], mean)


def outer_second_kernel(scale, slots, place, grads_ref, mates_ref, stacked_ref, stacked_mate_ref, *refs):
    a_outs, b_outs, (block_ref, sems) = refs[-10:-6], refs[-6:-2], refs[-2:]
    row = lax.broadcasted_iota(jnp.int32, (UNITS, UNITS // 2), 0)
    col = lax.broadcasted_iota(jnp.int32, (UNITS, UNITS // 2), 1)
    wanted = (col >> 6) * 128 + place.core * 64 + (col & 63)
    keep = jnp.where(row == wanted, 1.0, 0.0).astype(BF16)
    copies = []
    for index, slot in enumerate(slots):
        mine = mm(grads_ref[index], keep).astype(BF16)
        other = mm(mates_ref[index], keep).astype(BF16)
        total = mm_first(mine, stacked_ref[...]) + mm_first(other, stacked_mate_ref[...])
        total = (total * scale).astype(BF16)
        block_ref[index, 0] = total[:, :UNITS].reshape(HID, 64, UNITS)
        block_ref[index, 1] = total[:, UNITS:].reshape(HID, 64, UNITS)
        for d, out in enumerate(a_outs):
            copies.append(pltpu.make_async_copy(
                block_ref.at[index, 0, lax.rem(place.z + d, HID)], out.at[slot], sems.at[index, d]
            ))
            copies[-1].start()
        step = lax.rem(place.hid + 2 * HID - place.x - slot, HID)
        for d, out in enumerate(b_outs):

            @pl.when(step == d)
            def _():
                pltpu.make_async_copy(block_ref.at[index, 1], out, sems.at[index, HID]).start()

    for index, slot in enumerate(slots):
        pltpu.make_async_copy(block_ref.at[index, 1], b_outs[0], sems.at[index, HID]).wait()
    for copy in copies:
        copy.wait()


def middle_kernel(place, a0, a1, a2, a3, b0, b1, b2, b3, c0, c1, c2, c3, d0, d1, d2, d3, total_ref):
    total_ref[0] = a0[...].astype(F32) + a1[...].astype(F32) + a2[...].astype(F32) + a3[...].astype(F32)
    total_ref[1] = b0[...].astype(F32) + b1[...].astype(F32) + b2[...].astype(F32) + b3[...].astype(F32)
    for d, out in enumerate((c0, c1, c2, c3)):
        out[...] = total_ref[0, lax.rem(place.hid + 2 * HID - place.x - d, HID)].astype(out.dtype)
    for d, out in enumerate((d0, d1, d2, d3)):
        out[...] = total_ref[1, lax.rem(place.z + d, HID)].astype(out.dtype)


def last_second_kernel(c0, c1, c2, c3, d0, d1, d2, d3, out_ref):
    for half, parts in enumerate(((c0, c1, c2, c3), (d0, d1, d2, d3))):
        total = parts[0][...]
        for part in parts[1:]:
            total = total + part[...].astype(F32)
        out_ref[:, half, :] = total


def settle_kernel(
    place, back_ref, own_ref, slope_ref, selt_ref, w_ref, grad_ref, mine_ref, s1, s2, s3, full_ref
):
    me = place.hid
    grad = own_ref[...] + mm(selt_ref[...], back_ref[...].reshape(FAR, UNITS))
    grad = (grad * slope_ref[...]).astype(BF16)
    grad_ref[...] = grad
    full_ref[...] = mm_last(grad, w_ref[...])
    for d, out in ((2, s2), (1, s1), (3, s3), (0, mine_ref)):
        target = lax.rem(me + d, HID)
        for half, base in ((1, 0), (0, UNITS)):
            cols = pl.ds(pl.multiple_of(base + target * LANES, LANES), LANES)
            out[:, half * LANES : (half + 1) * LANES] = full_ref[:, cols].astype(out.dtype)


def outer_first_kernel(scale, both_ref, grad_ref, out_ref):
    product = (mm_first(both_ref[...], grad_ref[...]) * scale).astype(BF16)
    product = product.reshape(2, PEERS, SLOTS, UNITS)
    for part in range(HID):
        for kind in range(2):
            start = (part * 2 + kind) * SLOTS
            out_ref[:, start : start + SLOTS] = product[kind, :, :, part * LANES : (part + 1) * LANES]


def return_kernel(mine_ref, r1, r2, r3, inv_ref, adjt_ref, merged_ref, base_ref, out_ref, halo_ref, sem):
    total = mine_ref[...] + r1[...].astype(F32) + r2[...].astype(F32) + r3[...].astype(F32)
    mean = (total[:, :LANES] * inv_ref[...]).astype(BF16)
    halo_ref[...] = mm(adjt_ref[ROWS:, :], mean).astype(BF16).reshape(PEERS, SLOTS, LANES)
    copy = pltpu.make_async_copy(halo_ref, out_ref.at[:, pl.ds(LANES, SLOTS), :], sem)
    copy.start()
    base_ref[...] = total[:, LANES:] + mm(adjt_ref[:ROWS, :], mean)
    copy.wait()


def final_kernel(base_ref, selt_ref, parts_ref, feat_ref, weight_ref):
    back = parts_ref[:, LANES:].reshape(FAR, LANES)
    feat_ref[...] = base_ref[...] + mm(selt_ref[...], back)
    total = parts_ref[0, :LANES].astype(F32)
    for index in range(1, PEERS):
        total = total + parts_ref[index, :LANES].astype(F32)
    for part in range(HID):
        for kind in range(2):
            start = (part * 2 + kind) * SLOTS
            weight_ref[:, kind, part * LANES : (part + 1) * LANES] = total[start : start + SLOTS]


class Place:
    def __init__(self):
        node = lax.axis_index("nodes")
        self.hid = lax.axis_index("hid")
        self.core = node & 1
        self.x = node >> 3
        self.z = (node >> 1) & 3


class Late:
    def __init__(self, source, ref, sem):
        self.ref = ref
        self.source = source
        self.copy = pltpu.make_async_copy(source, ref, sem)
        self.copy.start()
        self.waited = False

    def __getitem__(self, index):
        if not self.waited:
            self.copy.wait()
            self.waited = True
        return self.ref[index]


def in_hbm(value):
    return pltpu.with_memory_space_constraint(value, pltpu.HBM)


def call(
    kernel, name, operands, outs, scratch=(), placed=False, scalars=0, after=(), late=(), held=(), stored=(),
    loose=(), aliases=None, work=1,
):
    shapes = [
        pltpu.HBM(shape, dtype) if index in (*stored, *loose) else jax.ShapeDtypeStruct(shape, dtype)
        for index, (shape, dtype) in enumerate(outs)
    ]
    operands = [in_hbm(o) if index in (*late, *held) else o for index, o in enumerate(operands)]
    count = len(operands)
    in_specs = [
        pl.BlockSpec(memory_space=pltpu.SMEM if index < scalars else pltpu.VMEM) for index in range(count)
    ] + [pl.BlockSpec(memory_space=pl.ANY)] * len(after)
    for index in (*late, *held, *(aliases or {})):
        in_specs[index] = pl.BlockSpec(memory_space=pltpu.HBM)
    out_specs = [
        pl.BlockSpec(memory_space=pltpu.HBM if index in (*stored, *loose) else pltpu.VMEM)
        for index in range(len(shapes))
    ]
    first_out = count + len(after)
    fixed = first_out + len(shapes) + len(scratch)
    buffers = [pltpu.VMEM(operands[index].shape, operands[index].dtype) for index in late]
    buffers += [pltpu.VMEM(*outs[index]) for index in stored]
    sems = [pltpu.SemaphoreType.DMA for _ in buffers]

    def body(*refs):
        inputs = list(refs[:count])
        outputs = list(refs[first_out : first_out + len(shapes)])
        spare, flags = refs[fixed : fixed + len(buffers)], refs[fixed + len(buffers) :]
        for slot, index in enumerate(late):
            inputs[index] = Late(inputs[index], spare[slot], flags[slot])
        copies = []
        for slot, index in enumerate(stored, len(late)):
            copies.append(pltpu.make_async_copy(spare[slot], outputs[index], flags[slot]))
            outputs[index] = spare[slot]
        kernel(*([Place()] if placed else []), *inputs, *outputs, *refs[first_out + len(shapes) : fixed])
        for copy in copies:
            copy.start()
        for copy in copies:
            copy.wait()

    moved = sum(o.size * o.dtype.itemsize for o in operands) + sum(
        math.prod(shape) * jnp.dtype(dtype).itemsize for shape, dtype in outs
    )
    results = pl.pallas_call(
        body,
        out_shape=shapes,
        in_specs=in_specs,
        out_specs=out_specs,
        scratch_shapes=list(scratch) + buffers + sems,
        input_output_aliases=aliases or {},
        compiler_params=pltpu.CompilerParams(vmem_limit_bytes=16 * 1024 * 1024),
        cost_estimate=pl.CostEstimate(flops=work * BIG, bytes_accessed=moved, transcendentals=0),
        name=name,
    )(*operands, *after)
    return results[0] if len(outs) == 1 else results


def around(values):
    return [lax.ppermute(v, "hid", [(i, (i + d) % HID) for i in range(HID)]) for d, v in values]


def node_at(x, z, core):
    return ((x % 4) * 4 + z % 4) * 2 + core


def swap(value):
    return lax.ppermute(value, "nodes", [(i, i ^ 1) for i in range(PEERS)])


def along_z(values):
    return [
        lax.ppermute(v, "nodes", [
            (node_at(x, z, c), node_at(x, z + d, c)) for x in range(4) for z in range(4) for c in range(2)
        ])
        for d, v in values
    ]


def along_x(values):
    return [
        lax.ppermute(v, "nodes", [
            (node_at(x, z, c), node_at(x + d, z, c)) for x in range(4) for z in range(4) for c in range(2)
        ])
        for d, v in values
    ]


def on_device(features, neighbors, degree, send_rows, node_count, w_first, w_second, cotangent):
    scale = float(ROWS * PEERS) ** (-0.5)
    routes = jnp.swapaxes(send_rows, 1, 2).reshape(SLOTS, PEERS)
    w1 = w_first.reshape(2 * UNITS, UNITS)
    w2 = w_second.reshape(2 * UNITS, HID * UNITS)
    chunk = ((ROWS, UNITS), BF16)

    wide_chunk = ((ROWS, UNITS), F32)
    halo = ((PEERS, SLOTS, UNITS), BF16)
    f2, f1, f3 = around([(2, features), (1, features), (3, features)])
    adj, adjt, inv, sel, selt = call(
        count_kernel, "count", (jnp.swapaxes(neighbors, 0, 1), degree.reshape(1, ROWS), routes),
        [
            ((ROWS, ROWS + FAR), BF16), ((ROWS + FAR, ROWS), BF16), ((ROWS, LANES), F32),
            ((FAR, ROWS), BF16), ((ROWS, FAR), BF16),
        ],
        scratch=[pltpu.VMEM((KEPT, ROWS), jnp.int32)] * 3, late=(2, 1, 0), stored=(4,), work=8,
    )
    full, send_feat = call(
        pick_kernel, "pick", (features, f1, f2, f3, sel), [chunk, halo], placed=True,
    )
    far_feat = lax.all_to_all(send_feat, "nodes", 0, 0, tiled=True)
    both, hidden, send_hidden = call(
        first_kernel, "first", (full, far_feat, adj, inv, w1, sel),
        [((ROWS, 2 * UNITS), BF16), chunk, halo], work=6,
    )
    far_hidden = lax.all_to_all(send_hidden, "nodes", 0, 0, tiled=True)
    stacked, own_pre, s1, s2, s3 = call(
        second_kernel, "second", (hidden, far_hidden, adj, inv, w2),
        [((ROWS, 2 * UNITS), BF16), wide_chunk] + [chunk] * 3, placed=True, work=10,
    )
    r2, r1, r3 = around([(2, s2), (1, s1), (3, s3)])
    slope, saved = call(
        gate_kernel, "gate", (both, stacked, w1), [wide_chunk, ((ROWS, 2 * UNITS), BF16)],
        after=(s1,), late=(2,), stored=(0, 1), work=2,
    )
    saved_mate = swap(saved)
    g0 = call(
        slope_kernel, "slope", (node_count, own_pre, r1, r2, r3, cotangent), [chunk], scalars=1,
        after=(in_hbm(slope),),
    )
    g2, g1, g3 = around([(2, g0), (1, g0), (3, g0)])

    def outer(slots, grads, held):
        return tuple(call(
            lambda *refs: outer_second_kernel(scale, slots, *refs), "outer_second",
            (grads, swap(grads), saved, saved_mate, *held),
            [((HID, 64, UNITS), BF16)] * 8,
            scratch=[
                pltpu.VMEM((len(slots), 2, HID, 64, UNITS), BF16),
                pltpu.SemaphoreType.DMA((len(slots), HID + 1)),
            ],
            placed=True, loose=tuple(range(8)), late=(2, 0, 3, 1),
            aliases={4 + index: index for index in range(8)} if held else None, work=3 * len(slots),
        ))

    z = outer((0,), g0.reshape(1, ROWS, UNITS), ())
    halo_hidden, own_hidden, others = call(
        spread_kernel, "spread", (g0, g1, g2, g3, w2, inv, adjt),
        [halo, wide_chunk, ((3, ROWS, UNITS), BF16)], placed=True, after=(in_hbm(z[0]),), work=10, stored=(2,),
    )
    back_hidden = lax.all_to_all(halo_hidden, "nodes", 0, 0, tiled=True)
    z = outer((1, 2, 3), others, z)
    a0, a1, a2, a3, b0, b1, b2, b3 = z
    a2, b2, a1, b1, a3, b3 = (
        along_z([(2, a2)]) + along_x([(2, b2)]) + along_z([(1, a1)]) + along_x([(1, b1)])
        + along_z([(3, a3)]) + along_x([(3, b3)])
    )
    c0, c1, c2, c3, d0, d1, d2, d3 = call(
        middle_kernel, "middle", (a0, a1, a2, a3, b0, b1, b2, b3),
        ([((64, UNITS), F32)] + [((64, UNITS), BF16)] * 3) * 2,
        scratch=[pltpu.VMEM((2, HID, 64, UNITS), F32)], placed=True, late=tuple(range(8)),
    )
    grad, mine, s1, s2, s3 = call(
        settle_kernel, "settle",
        (back_hidden, own_hidden, slope, selt, w1),
        [chunk, ((ROWS, 2 * LANES), F32)] + [((ROWS, 2 * LANES), BF16)] * 3,
        scratch=[pltpu.VMEM((ROWS, 2 * UNITS), F32)], placed=True, late=(3, 2, 4), work=6,
    )
    r2, r1, r3 = around([(2, s2), (1, s1), (3, s3)])
    merged = call(
        lambda *refs: outer_first_kernel(scale, *refs), "outer_first", (both, grad),
        [((PEERS, LANES + SLOTS, LANES), BF16)], after=(s1,), stored=(0,), work=2,
    )
    base, merged = call(
        return_kernel, "return", (mine, r1, r2, r3, inv, adjt, merged),
        [((ROWS, LANES), F32), ((PEERS, LANES + SLOTS, LANES), BF16)],
        scratch=[pltpu.VMEM((PEERS, SLOTS, LANES), BF16), pltpu.SemaphoreType.DMA],
        loose=(1,), aliases={6: 1}, after=(c0,),
    )
    parts = lax.all_to_all(merged, "nodes", 0, 0, tiled=True)
    c2, d2, c1, d1, c3, d3 = (
        along_x([(2, c2)]) + along_z([(2, d2)]) + along_x([(1, c1)]) + along_z([(1, d1)])
        + along_x([(3, c3)]) + along_z([(3, d3)])
    )
    grad_features, grad_w_first = call(
        final_kernel, "final", (base, selt, parts),
        [((ROWS, LANES), F32), ((SLOTS, 2, UNITS), F32)],
    )
    grad_w_second = call(last_second_kernel, "last_second", (c0, c1, c2, c3, d0, d1, d2, d3), [((64, 2, UNITS), F32)])
    return grad_w_first, grad_w_second, grad_features


def solution(mesh):
    placed = (
        P("nodes", "hid"),
        P("nodes", None),
        P("nodes"),
        P("nodes", None, None),
        P("nodes"),
        P(None, None, "hid"),
        P(None, "hid", None),
        P("nodes", "hid"),
    )
    return jax.shard_map(
        on_device,
        mesh=mesh,
        in_specs=placed,
        out_specs=(P("nodes", None, "hid"), P("nodes", None, "hid"), P("nodes", "hid")),
        check_vma=False,
    )
```

```python
import math

import jax
import jax.numpy as jnp
from jax import lax
from jax.experimental import pallas as pl
from jax.experimental.pallas import tpu as pltpu
from jax.sharding import PartitionSpec as P

BF16 = jnp.bfloat16
F32 = jnp.float32
ROWS = 256
PEERS = 32
SLOTS = 16
FAR = PEERS * SLOTS
HID = 4
LANES = 128
UNITS = 512
KEPT = 80
BIG = 2 * ROWS * UNITS * UNITS


def mm(left_op, right_op):
    return jnp.dot(left_op, right_op, preferred_element_type=F32)


def mm_last(left_op, right_op):
    return lax.dot_general(left_op, right_op, (((1,), (1,)), ((), ())), preferred_element_type=F32)


def mm_first(left_op, right_op):
    return lax.dot_general(left_op, right_op, (((0,), (0,)), ((), ())), preferred_element_type=F32)


def wide(column, width):
    return jnp.concatenate([column] * (width // LANES), axis=1)


def route_rows(routes_ref):
    peer = lax.broadcasted_iota(jnp.int32, (PEERS, FAR), 0)
    lane_peer = lax.broadcasted_iota(jnp.int32, (PEERS, FAR), 1) >> 4
    spread_out = jnp.where(peer == lane_peer, 1.0, 0.0).astype(BF16)
    by_slot = mm(routes_ref[...].astype(F32).astype(BF16), spread_out)
    slot = lax.broadcasted_iota(jnp.int32, (SLOTS, FAR), 0)
    lane_slot = lax.broadcasted_iota(jnp.int32, (SLOTS, FAR), 1) & (SLOTS - 1)
    routes = jnp.sum(jnp.where(slot == lane_slot, by_slot, 0.0), axis=0, keepdims=True)
    row = lax.broadcasted_iota(jnp.int32, (ROWS, FAR), 0).astype(F32)
    return jnp.where(row == routes, 1.0, 0.0)


def pick_kernel(routes_ref, feat_ref, sel_ref, send_ref):
    sel = route_rows(routes_ref).T.astype(BF16)
    sel_ref[...] = sel
    picked = mm(sel, feat_ref[...]).astype(BF16).reshape(PEERS, SLOTS, LANES)
    for part in range(HID):
        send_ref[:, part] = picked


def count_kernel(
    neigh_ref, degree_ref, routes_ref, adj_ref, adjt_ref, inv_ref, selt_ref, key_ref, low_ref, high_ref
):
    selt_ref[...] = route_rows(routes_ref).astype(BF16)
    inv_ref[...] = 1.0 / jnp.broadcast_to(degree_ref[...].astype(F32), (LANES, ROWS)).T
    entry = neigh_ref[...]
    used = lax.broadcasted_iota(jnp.int32, (KEPT, ROWS), 0) < degree_ref[...]
    block = entry >> 7
    upper = block >= 3
    weight = jnp.where(used, jnp.left_shift(1, 10 * jnp.where(upper, block - 3, block)), 0)
    key_ref[...] = entry & (LANES - 1)
    low_ref[...] = jnp.where(upper, 0, weight)
    high_ref[...] = jnp.where(upper, weight, 0)
    tall = 64
    for half in range(LANES // tall):
        value = lax.broadcasted_iota(jnp.int32, (tall, LANES), 0) + half * tall
        for side in range(ROWS // LANES):
            cols = slice(side * LANES, (side + 1) * LANES)

            def step(index, carry):
                low, high = carry
                at = pl.ds(pl.multiple_of(index * 8, 8), 8)
                keys, lows, highs = key_ref[at, cols], low_ref[at, cols], high_ref[at, cols]
                for j in range(8):
                    same = keys[j : j + 1] == value
                    low = low + jnp.where(same, lows[j : j + 1], 0)
                    high = high + jnp.where(same, highs[j : j + 1], 0)
                return low, high

            empty = jnp.zeros((tall, LANES), jnp.int32)
            low, high = lax.fori_loop(0, KEPT // 8, step, (empty, empty))
            for t in range(3):
                for base, packed in ((0, low), (3, high)):
                    count = jnp.right_shift(packed, 10 * t) & 1023
                    start = (base + t) * LANES + half * tall
                    adjt_ref[start : start + tall, cols] = count.astype(F32).astype(BF16)
    for t in range((ROWS + FAR) // LANES):
        rows = slice(t * LANES, (t + 1) * LANES)
        adj_ref[:, rows] = adjt_ref[rows, :].astype(F32).T.astype(BF16)


def first_kernel(
    place, f0, f1, f2, f3, far_ref, adj_ref, inv_ref, w_ref, sel_ref, both_ref, hidden_ref, send_ref, far_all
):
    for d, piece in enumerate((f0, f1, f2, f3)):
        origin = lax.rem(place.hid + HID - d, HID)
        both_ref[:, pl.ds(pl.multiple_of(origin * LANES, LANES), LANES)] = piece[...]
    for origin in range(HID):
        far_all[:, origin * LANES : (origin + 1) * LANES] = far_ref[:, origin].reshape(FAR, LANES)
    agg = mm(adj_ref[:, :ROWS], both_ref[:, :UNITS]) + mm(adj_ref[:, ROWS:], far_all[...])
    both_ref[:, UNITS:] = (agg * wide(inv_ref[...], UNITS)).astype(BF16)
    pre = mm(both_ref[...], w_ref[...])
    sig = 1.0 / (1.0 + jnp.exp(-pre))
    hidden = (pre * sig).astype(BF16)
    hidden_ref[...] = hidden
    send_ref[...] = mm(sel_ref[...], hidden).astype(BF16).reshape(PEERS, SLOTS, UNITS)


def gate_kernel(both_ref, stacked_ref, w1_ref, slope_ref, saved_ref):
    saved_ref[...] = stacked_ref[...]
    pre = mm(both_ref[...], w1_ref[...])
    sig = 1.0 / (1.0 + jnp.exp(-pre))
    slope_ref[...] = sig * (1.0 + pre * (1.0 - sig))


def second_kernel(
    place, hidden_ref, far_ref, adj_ref, inv_ref, w_hbm, stacked_ref,
    own_a, own_b, s1a, s1b, s2a, s2b, s3a, s3b, w_ref, sems,
):
    order = ((2, s2a, s2b), (1, s1a, s1b), (3, s3a, s3b), (0, own_a, own_b))
    copies = []
    for slot, (d, upper, lower) in enumerate(order):
        target = lax.rem(place.hid + d, HID)
        cols = pl.ds(pl.multiple_of(target * UNITS, UNITS), UNITS)
        copies.append(pltpu.make_async_copy(w_hbm.at[:, cols], w_ref.at[slot], sems.at[slot]))
        copies[-1].start()
    hidden = hidden_ref[...]
    total = mm(adj_ref[:, :ROWS], hidden) + mm(adj_ref[:, ROWS:], far_ref[...].reshape(FAR, UNITS))
    stacked_ref[:, :UNITS] = hidden
    stacked_ref[:, UNITS:] = (total * wide(inv_ref[...], UNITS)).astype(BF16)
    for slot, (d, upper, lower) in enumerate(order):
        copies[slot].wait()
        part = mm(stacked_ref[...], w_ref[slot]).astype(upper.dtype)
        upper[...] = part[: ROWS // 2]
        lower[...] = part[ROWS // 2 :]


def slope_kernel(first_row, count_ref, own_ref, r1, r2, r3, cot_ref, grad_ref):
    pre = own_ref[...] + r1[...].astype(F32) + r2[...].astype(F32) + r3[...].astype(F32)
    sig = 1.0 / (1.0 + jnp.exp(-pre))
    slope = cot_ref[first_row : first_row + ROWS // 2, :].astype(F32) * (sig * (1.0 + pre * (1.0 - sig)))
    live = lax.broadcasted_iota(jnp.int32, pre.shape, 0) + first_row < count_ref[0]
    grad_ref[...] = jnp.where(live, slope, 0.0).astype(BF16)


def spread_kernel(
    place, g0a, g0b, g1a, g1b, g2a, g2b, g3a, g3b, w_ref, inv_ref, adjt_ref, halo_ref, own_hbm, others_ref,
    own_ref, sems,
):
    parts = ((g0a, g0b), (g1a, g1b), (g2a, g2b), (g3a, g3b))
    rows = ROWS // 2
    copies = [
        pltpu.make_async_copy(ref, others_ref.at[d, pl.ds(half * rows, rows)], sems.at[2 * d + half])
        for d, pair in enumerate(parts)
        for half, ref in enumerate(pair)
    ]
    for copy in copies:
        copy.start()
    grads = {d: jnp.concatenate([upper[...], lower[...]], axis=0) for d, (upper, lower) in enumerate(parts)}

    def back(base):
        total = None
        for d in (0, 3, 1, 2):
            origin = lax.rem(place.hid + HID - d, HID)
            cols = pl.ds(pl.multiple_of(origin * UNITS, UNITS), UNITS)
            term = mm_last(grads[d], w_ref[base : base + UNITS, cols])
            total = term if total is None else total + term
        return total

    mean = (back(UNITS) * wide(inv_ref[...], UNITS)).astype(BF16)
    own_ref[...] = back(0) + mm(adjt_ref[:ROWS, :], mean)
    copies.append(pltpu.make_async_copy(own_ref, own_hbm, sems.at[8]))
    copies[-1].start()
    halo_ref[...] = mm(adjt_ref[ROWS:, :], mean).astype(BF16).reshape(PEERS, SLOTS, UNITS)
    for copy in copies:
        copy.wait()


def outer_second_kernel(scale, slots, place, grads_ref, mates_ref, stacked_ref, stacked_mate_ref, *refs):
    outs, (block_ref, sems) = refs[-6:-2], refs[-2:]
    row = lax.broadcasted_iota(jnp.int32, (UNITS, UNITS // 2), 0)
    col = lax.broadcasted_iota(jnp.int32, (UNITS, UNITS // 2), 1)
    wanted = (col >> 6) * 128 + place.core * 64 + (col & 63)
    keep = jnp.where(row == wanted, 1.0, 0.0).astype(BF16)
    for index, slot in enumerate(slots):
        mine = mm(grads_ref[index], keep).astype(BF16)
        other = mm(mates_ref[index], keep).astype(BF16)
        total = mm_first(mine, stacked_ref[...]) + mm_first(other, stacked_mate_ref[...])
        block_ref[index] = (total * scale).astype(BF16).reshape(HID, 64, 2 * UNITS)

        @pl.when(place.core == 0)
        def _():
            for d, out in enumerate(outs):
                source = block_ref.at[index, lax.rem(place.z + d, HID)]
                pltpu.make_async_copy(source, out.at[slot], sems.at[index, d]).start()

        step = lax.rem(place.hid + 2 * HID - place.x - slot, HID)
        for d, out in enumerate(outs):

            @pl.when((place.core == 1) & (step == d))
            def _():
                for z in range(HID):
                    pltpu.make_async_copy(block_ref.at[index, z], out.at[z], sems.at[index, z]).start()

    for index, slot in enumerate(slots):
        for d, out in enumerate(outs):
            pltpu.make_async_copy(block_ref.at[index, d], out.at[slot], sems.at[index, d]).wait()


def along_kernel(place, z0, z1, z2, z3, x0, x1, x2, x3):
    for d, out in enumerate((x0, x1, x2, x3)):
        by_x = lax.rem(place.hid + 2 * HID - place.x - d, HID)
        at = jnp.where(place.core == 0, by_x, lax.rem(place.z + d, HID))
        total = z0[at].astype(F32) + z1[at].astype(F32) + z2[at].astype(F32) + z3[at].astype(F32)
        out[...] = total.astype(out.dtype)


def last_second_kernel(x0, x1, x2, x3, out_ref):
    total = x0[...] + x1[...].astype(F32) + x2[...].astype(F32) + x3[...].astype(F32)
    out_ref[:, 0, :] = total[:, :UNITS]
    out_ref[:, 1, :] = total[:, UNITS:]


def settle_kernel(
    place, back_ref, own_ref, slope_ref, selt_ref, w_ref, grad_ref, mine_ref, s1, s2, s3, full_ref
):
    me = place.hid
    grad = own_ref[...] + mm(selt_ref[...], back_ref[...].reshape(FAR, UNITS))
    grad = (grad * slope_ref[...]).astype(BF16)
    grad_ref[...] = grad
    full_ref[...] = mm_last(grad, w_ref[...])
    for d, out in ((2, s2), (1, s1), (3, s3), (0, mine_ref)):
        target = lax.rem(me + d, HID)
        for half, base in ((1, 0), (0, UNITS)):
            cols = pl.ds(pl.multiple_of(base + target * LANES, LANES), LANES)
            out[:, half * LANES : (half + 1) * LANES] = full_ref[:, cols].astype(out.dtype)


def outer_first_kernel(scale, both_ref, grad_ref, out_ref):
    product = (mm_first(both_ref[...], grad_ref[...]) * scale).astype(BF16)
    product = product.reshape(2, PEERS, SLOTS, UNITS)
    for part in range(HID):
        for kind in range(2):
            start = (part * 2 + kind) * SLOTS
            out_ref[:, start : start + SLOTS] = product[kind, :, :, part * LANES : (part + 1) * LANES]


def return_kernel(mine_ref, r1, r2, r3, inv_ref, adjt_ref, merged_ref, base_ref, out_ref, halo_ref, sem):
    total = mine_ref[...] + r1[...].astype(F32) + r2[...].astype(F32) + r3[...].astype(F32)
    mean = (total[:, :LANES] * inv_ref[...]).astype(BF16)
    halo_ref[...] = mm(adjt_ref[ROWS:, :], mean).astype(BF16).reshape(PEERS, SLOTS, LANES)
    copy = pltpu.make_async_copy(halo_ref, out_ref.at[:, pl.ds(LANES, SLOTS), :], sem)
    copy.start()
    base_ref[...] = total[:, LANES:] + mm(adjt_ref[:ROWS, :], mean)
    copy.wait()


def final_kernel(base_ref, selt_ref, parts_ref, feat_ref, weight_ref):
    back = parts_ref[:, LANES:].reshape(FAR, LANES)
    feat_ref[...] = base_ref[...] + mm(selt_ref[...], back)
    total = parts_ref[0, :LANES].astype(F32)
    for index in range(1, PEERS):
        total = total + parts_ref[index, :LANES].astype(F32)
    for part in range(HID):
        for kind in range(2):
            start = (part * 2 + kind) * SLOTS
            weight_ref[:, kind, part * LANES : (part + 1) * LANES] = total[start : start + SLOTS]


class Place:
    def __init__(self):
        node = lax.axis_index("nodes")
        self.hid = lax.axis_index("hid")
        self.core = node & 1
        self.x = node >> 3
        self.z = (node >> 1) & 3


class Late:
    def __init__(self, source, ref, sem):
        self.ref = ref
        self.source = source
        self.copy = pltpu.make_async_copy(source, ref, sem)
        self.copy.start()
        self.waited = False

    def __getitem__(self, index):
        if not self.waited:
            self.copy.wait()
            self.waited = True
        return self.ref[index]


def in_hbm(value):
    return pltpu.with_memory_space_constraint(value, pltpu.HBM)


def call(
    kernel, name, operands, outs, scratch=(), placed=False, scalars=0, after=(), late=(), held=(), stored=(),
    loose=(), aliases=None, work=1,
):
    shapes = [
        pltpu.HBM(shape, dtype) if index in (*stored, *loose) else jax.ShapeDtypeStruct(shape, dtype)
        for index, (shape, dtype) in enumerate(outs)
    ]
    operands = [in_hbm(o) if index in (*late, *held) else o for index, o in enumerate(operands)]
    count = len(operands)
    in_specs = [
        pl.BlockSpec(memory_space=pltpu.SMEM if index < scalars else pltpu.VMEM) for index in range(count)
    ] + [pl.BlockSpec(memory_space=pl.ANY)] * len(after)
    for index in (*late, *held, *(aliases or {})):
        in_specs[index] = pl.BlockSpec(memory_space=pltpu.HBM)
    out_specs = [
        pl.BlockSpec(memory_space=pltpu.HBM if index in (*stored, *loose) else pltpu.VMEM)
        for index in range(len(shapes))
    ]
    first_out = count + len(after)
    fixed = first_out + len(shapes) + len(scratch)
    buffers = [pltpu.VMEM(operands[index].shape, operands[index].dtype) for index in late]
    buffers += [pltpu.VMEM(*outs[index]) for index in stored]
    sems = [pltpu.SemaphoreType.DMA for _ in buffers]

    def body(*refs):
        inputs = list(refs[:count])
        outputs = list(refs[first_out : first_out + len(shapes)])
        spare, flags = refs[fixed : fixed + len(buffers)], refs[fixed + len(buffers) :]
        for slot, index in enumerate(late):
            inputs[index] = Late(inputs[index], spare[slot], flags[slot])
        copies = []
        for slot, index in enumerate(stored, len(late)):
            copies.append(pltpu.make_async_copy(spare[slot], outputs[index], flags[slot]))
            outputs[index] = spare[slot]
        kernel(*([Place()] if placed else []), *inputs, *outputs, *refs[first_out + len(shapes) : fixed])
        for copy in copies:
            copy.start()
        for copy in copies:
            copy.wait()

    moved = sum(o.size * o.dtype.itemsize for o in operands) + sum(
        math.prod(shape) * jnp.dtype(dtype).itemsize for shape, dtype in outs
    )
    results = pl.pallas_call(
        body,
        out_shape=shapes,
        in_specs=in_specs,
        out_specs=out_specs,
        scratch_shapes=list(scratch) + buffers + sems,
        input_output_aliases=aliases or {},
        compiler_params=pltpu.CompilerParams(vmem_limit_bytes=16 * 1024 * 1024),
        cost_estimate=pl.CostEstimate(flops=work * BIG, bytes_accessed=moved, transcendentals=0),
        name=name,
    )(*operands, *after)
    return results[0] if len(outs) == 1 else results


def around(values):
    return [lax.ppermute(v, "hid", [(i, (i + d) % HID) for i in range(HID)]) for d, v in values]


def node_at(x, z, core):
    return ((x % 4) * 4 + z % 4) * 2 + core


def swap(value):
    return lax.ppermute(value, "nodes", [(i, i ^ 1) for i in range(PEERS)])


def near(values, turned):
    def target(x, z, core, d):
        return node_at(x, z + d, core) if (core == 0) != turned else node_at(x + d, z, core)

    return [
        lax.ppermute(v, "nodes", [
            (node_at(x, z, c), target(x, z, c, d)) for x in range(4) for z in range(4) for c in range(2)
        ])
        for d, v in values
    ]


def on_device(features, neighbors, degree, send_rows, node_count, w_first, w_second, cotangent):
    scale = float(ROWS * PEERS) ** (-0.5)
    routes = jnp.swapaxes(send_rows, 1, 2).reshape(SLOTS, PEERS)
    w1 = w_first.reshape(2 * UNITS, UNITS)
    w2 = w_second.reshape(2 * UNITS, HID * UNITS)
    chunk = ((ROWS, UNITS), BF16)

    wide_chunk = ((ROWS, UNITS), F32)
    halo = ((PEERS, SLOTS, UNITS), BF16)
    sel, send_feat = call(
        pick_kernel, "pick", (routes, features),
        [((FAR, ROWS), BF16), ((PEERS, HID, SLOTS, LANES), BF16)], late=(0, 1), work=1,
    )
    far_feat = lax.all_to_all(
        send_feat.reshape(PEERS * HID, SLOTS, LANES), ("nodes", "hid"), 0, 0, tiled=True
    ).reshape(PEERS, HID, SLOTS, LANES)
    f2, f1, f3 = around([(2, features), (1, features), (3, features)])
    adj, adjt, inv, selt = call(
        count_kernel, "count", (jnp.swapaxes(neighbors, 0, 1), degree.reshape(1, ROWS), routes),
        [
            ((ROWS, ROWS + FAR), BF16), ((ROWS + FAR, ROWS), BF16), ((ROWS, LANES), F32), ((ROWS, FAR), BF16),
        ],
        scratch=[pltpu.VMEM((KEPT, ROWS), jnp.int32)] * 3, late=(2, 1, 0), stored=(3,), work=8, after=(sel,),
    )
    both, hidden, send_hidden = call(
        first_kernel, "first", (features, f1, f2, f3, far_feat, adj, inv, w1, sel),
        [((ROWS, 2 * UNITS), BF16), chunk, halo], work=6, placed=True,
        scratch=[pltpu.VMEM((FAR, UNITS), BF16)],
    )
    far_hidden = lax.all_to_all(send_hidden, "nodes", 0, 0, tiled=True)
    half_chunk = ((ROWS // 2, UNITS), BF16)
    stacked, own_a, own_b, s1a, s1b, s2a, s2b, s3a, s3b = call(
        second_kernel, "second", (hidden, far_hidden, adj, inv, w2),
        [((ROWS, 2 * UNITS), BF16)] + [((ROWS // 2, UNITS), F32)] * 2 + [half_chunk] * 6,
        scratch=[pltpu.VMEM((HID, 2 * UNITS, UNITS), BF16), pltpu.SemaphoreType.DMA((HID,))],
        placed=True, work=10, held=(4,),
    )
    r2a, r1a, r3a = around([(2, s2a), (1, s1a), (3, s3a)])
    r2b, r1b, r3b = around([(2, s2b), (1, s1b), (3, s3b)])
    slope, saved = call(
        gate_kernel, "gate", (both, stacked, w1), [wide_chunk, ((ROWS, 2 * UNITS), BF16)],
        after=(s1a,), late=(2,), stored=(0, 1), work=2,
    )
    saved_mate = swap(saved)
    def gradient(first_row, own, parts):
        return call(
            lambda *refs: slope_kernel(first_row, *refs), "slope", (node_count, own, *parts, cotangent),
            [half_chunk], scalars=1, after=(in_hbm(slope),),
        )

    g0a = gradient(0, own_a, (r1a, r2a, r3a))
    g2a, g1a, g3a = around([(2, g0a), (1, g0a), (3, g0a)])
    g0b = gradient(ROWS // 2, own_b, (r1b, r2b, r3b))
    g2b, g1b, g3b = around([(2, g0b), (1, g0b), (3, g0b)])

    def outer(slots, grads, held, late):
        return tuple(call(
            lambda *refs: outer_second_kernel(scale, slots, *refs), "outer_second",
            (grads, swap(grads), saved, saved_mate, *held),
            [((HID, 64, 2 * UNITS), BF16)] * HID,
            scratch=[
                pltpu.VMEM((len(slots), HID, 64, 2 * UNITS), BF16),
                pltpu.SemaphoreType.DMA((len(slots), HID)),
            ],
            placed=True, loose=tuple(range(HID)), late=late,
            aliases={4 + index: index for index in range(HID)} if held else None, work=3 * len(slots),
        ))

    halo_hidden, own_hidden, others = call(
        spread_kernel, "spread", (g0a, g0b, g1a, g1b, g2a, g2b, g3a, g3b, w2, inv, adjt),
        [halo, wide_chunk, ((HID, ROWS, UNITS), BF16)], placed=True, work=10, loose=(1, 2),
        scratch=[pltpu.VMEM((ROWS, UNITS), F32), pltpu.SemaphoreType.DMA((9,))],
    )
    back_hidden = lax.all_to_all(halo_hidden, "nodes", 0, 0, tiled=True)
    z0, z1, z2, z3 = outer((0, 1, 2, 3), others, (), (0, 2, 3))
    outer_done = in_hbm(z0)
    z2, z1, z3 = near([(2, z2), (1, z1), (3, z3)], False)
    grad, mine, s1, s2, s3 = call(
        settle_kernel, "settle",
        (back_hidden, own_hidden, slope, selt, w1),
        [chunk, ((ROWS, 2 * LANES), F32)] + [((ROWS, 2 * LANES), BF16)] * 3,
        scratch=[pltpu.VMEM((ROWS, 2 * UNITS), F32)], placed=True, late=(3, 1, 2, 4), work=6, after=(outer_done,),
    )
    r2, r1, r3 = around([(2, s2), (1, s1), (3, s3)])
    merged = call(
        lambda *refs: outer_first_kernel(scale, *refs), "outer_first", (both, grad),
        [((PEERS, LANES + SLOTS, LANES), BF16)], after=(s1,), stored=(0,), work=2,
    )
    x0, x1, x2, x3 = call(
        along_kernel, "along", (z0, z1, z2, z3),
        [((64, 2 * UNITS), F32)] + [((64, 2 * UNITS), BF16)] * 3, placed=True, late=(0,), after=(s1,),
    )
    base, merged = call(
        return_kernel, "return", (mine, r1, r2, r3, inv, adjt, merged),
        [((ROWS, LANES), F32), ((PEERS, LANES + SLOTS, LANES), BF16)],
        scratch=[pltpu.VMEM((PEERS, SLOTS, LANES), BF16), pltpu.SemaphoreType.DMA],
        loose=(1,), aliases={6: 1}, after=(x0,),
    )
    parts = lax.all_to_all(merged, "nodes", 0, 0, tiled=True)
    x2, x1, x3 = near([(2, x2), (1, x1), (3, x3)], True)
    grad_features, grad_w_first = call(
        final_kernel, "final", (base, selt, parts),
        [((ROWS, LANES), F32), ((SLOTS, 2, UNITS), F32)],
    )
    grad_w_second = call(last_second_kernel, "last_second", (x0, x1, x2, x3), [((64, 2, UNITS), F32)])
    return grad_w_first, grad_w_second, grad_features


def solution(mesh):
    placed = (
        P("nodes", "hid"),
        P("nodes", None),
        P("nodes"),
        P("nodes", None, None),
        P("nodes"),
        P(None, None, "hid"),
        P(None, "hid", None),
        P("nodes", "hid"),
    )
    return jax.shard_map(
        on_device,
        mesh=mesh,
        in_specs=placed,
        out_specs=(P("nodes", None, "hid"), P("nodes", None, "hid"), P("nodes", "hid")),
        check_vma=False,
    )
```

```python
import math

import jax
import jax.numpy as jnp
from jax import lax
from jax.experimental import pallas as pl
from jax.experimental.pallas import tpu as pltpu
from jax.sharding import PartitionSpec as P

BF16 = jnp.bfloat16
F32 = jnp.float32
ROWS = 256
PEERS = 32
SLOTS = 16
FAR = PEERS * SLOTS
HID = 4
LANES = 128
UNITS = 512
KEPT = 80
CHIPS = 16
BIG = 2 * ROWS * UNITS * UNITS


def mm(left_op, right_op):
    return jnp.dot(left_op, right_op, preferred_element_type=F32)


def mm_last(left_op, right_op):
    return lax.dot_general(left_op, right_op, (((1,), (1,)), ((), ())), preferred_element_type=F32)


def mm_first(left_op, right_op):
    return lax.dot_general(left_op, right_op, (((0,), (0,)), ((), ())), preferred_element_type=F32)


def wide(column, width):
    return jnp.concatenate([column] * (width // LANES), axis=1)


def route_rows(routes_ref):
    peer = lax.broadcasted_iota(jnp.int32, (PEERS, FAR), 0)
    lane_peer = lax.broadcasted_iota(jnp.int32, (PEERS, FAR), 1) >> 4
    spread_out = jnp.where(peer == lane_peer, 1.0, 0.0).astype(BF16)
    by_slot = mm(routes_ref[...].astype(F32).astype(BF16), spread_out)
    slot = lax.broadcasted_iota(jnp.int32, (SLOTS, FAR), 0)
    lane_slot = lax.broadcasted_iota(jnp.int32, (SLOTS, FAR), 1) & (SLOTS - 1)
    routes = jnp.sum(jnp.where(slot == lane_slot, by_slot, 0.0), axis=0, keepdims=True)
    row = lax.broadcasted_iota(jnp.int32, (ROWS, FAR), 0).astype(F32)
    return jnp.where(row == routes, 1.0, 0.0)


def pick_kernel(routes_ref, feat_ref, sel_ref, send_ref):
    sel = route_rows(routes_ref).T.astype(BF16)
    sel_ref[...] = sel
    picked = mm(sel, feat_ref[...]).astype(BF16).reshape(PEERS, SLOTS, LANES)
    for part in range(HID):
        send_ref[:, part] = picked


def count_kernel(
    neigh_ref, degree_ref, adj_ref, adjt_ref, inv_ref, key_ref, low_ref, high_ref
):
    inv_ref[...] = 1.0 / jnp.broadcast_to(degree_ref[...].astype(F32), (LANES, ROWS)).T
    entry = neigh_ref[...]
    used = lax.broadcasted_iota(jnp.int32, (KEPT, ROWS), 0) < degree_ref[...]
    block = entry >> 7
    upper = block >= 3
    weight = jnp.where(used, jnp.left_shift(1, 10 * jnp.where(upper, block - 3, block)), 0)
    key_ref[...] = entry & (LANES - 1)
    low_ref[...] = jnp.where(upper, 0, weight)
    high_ref[...] = jnp.where(upper, weight, 0)
    tall = 64
    for half in range(LANES // tall):
        value = lax.broadcasted_iota(jnp.int32, (tall, LANES), 0) + half * tall
        for side in range(ROWS // LANES):
            cols = slice(side * LANES, (side + 1) * LANES)

            def step(index, carry):
                low, high = carry
                at = pl.ds(pl.multiple_of(index * 8, 8), 8)
                keys, lows, highs = key_ref[at, cols], low_ref[at, cols], high_ref[at, cols]
                for j in range(8):
                    same = keys[j : j + 1] == value
                    low = low + jnp.where(same, lows[j : j + 1], 0)
                    high = high + jnp.where(same, highs[j : j + 1], 0)
                return low, high

            empty = jnp.zeros((tall, LANES), jnp.int32)
            low, high = lax.fori_loop(0, KEPT // 8, step, (empty, empty))
            for t in range(3):
                for base, packed in ((0, low), (3, high)):
                    count = jnp.right_shift(packed, 10 * t) & 1023
                    start = (base + t) * LANES + half * tall
                    adjt_ref[start : start + tall, cols] = count.astype(F32).astype(BF16)
    for t in range((ROWS + FAR) // LANES):
        rows = slice(t * LANES, (t + 1) * LANES)
        adj_ref[:, rows] = adjt_ref[rows, :].astype(F32).T.astype(BF16)


def first_kernel(
    place, f0, f1, f2, f3, far_ref, adj_ref, inv_ref, w_ref, sel_ref, both_ref, hidden_ref, send_ref, far_all
):
    for d, piece in enumerate((f0, f1, f2, f3)):
        origin = lax.rem(place.hid + HID - d, HID)
        both_ref[:, pl.ds(pl.multiple_of(origin * LANES, LANES), LANES)] = piece[...]
    for origin in range(HID):
        far_all[:, origin * LANES : (origin + 1) * LANES] = far_ref[:, origin].reshape(FAR, LANES)
    agg = mm(adj_ref[:, :ROWS], both_ref[:, :UNITS]) + mm(adj_ref[:, ROWS:], far_all[...])
    both_ref[:, UNITS:] = (agg * wide(inv_ref[...], UNITS)).astype(BF16)
    pre = mm(both_ref[...], w_ref[...])
    sig = 1.0 / (1.0 + jnp.exp(-pre))
    hidden = (pre * sig).astype(BF16)
    hidden_ref[...] = hidden
    send_ref[...] = mm(sel_ref[...], hidden).astype(BF16).reshape(PEERS, SLOTS, UNITS)


def gate_kernel(both_ref, stacked_ref, w1_ref, routes_ref, slope_ref, saved_ref, selt_ref):
    selt_ref[...] = route_rows(routes_ref).astype(BF16)
    saved_ref[...] = stacked_ref[...]
    pre = mm(both_ref[...], w1_ref[...])
    sig = 1.0 / (1.0 + jnp.exp(-pre))
    slope_ref[...] = sig * (1.0 + pre * (1.0 - sig))


def second_kernel(
    place, hidden_ref, far_ref, adj_ref, inv_ref, w_hbm, stacked_ref,
    own_a, own_b, s1a, s1b, s2a, s2b, s3a, s3b, w_ref, sems,
):
    order = ((2, s2a, s2b), (1, s1a, s1b), (3, s3a, s3b), (0, own_a, own_b))
    pieces, tall = 4, 2 * UNITS // 4
    copies = []
    for slot, (d, upper, lower) in enumerate(order):
        target = lax.rem(place.hid + d, HID)
        cols = pl.ds(pl.multiple_of(target * UNITS, UNITS), UNITS)
        for piece in range(pieces):
            rows = pl.ds(piece * tall, tall)
            copies.append(pltpu.make_async_copy(w_hbm.at[rows, cols], w_ref.at[slot, rows], sems.at[slot, piece]))
            copies[-1].start()
    hidden = hidden_ref[...]
    total = mm(adj_ref[:, :ROWS], hidden) + mm(adj_ref[:, ROWS:], far_ref[...].reshape(FAR, UNITS))
    stacked_ref[:, :UNITS] = hidden
    stacked_ref[:, UNITS:] = (total * wide(inv_ref[...], UNITS)).astype(BF16)
    for slot, (d, upper, lower) in enumerate(order):
        for copy in copies[slot * pieces : (slot + 1) * pieces]:
            copy.wait()
        part = mm(stacked_ref[...], w_ref[slot]).astype(upper.dtype)
        upper[...] = part[: ROWS // 2]
        lower[...] = part[ROWS // 2 :]


def choose_kernel(place, both_ref, mine_ref, give_ref):
    row = lax.broadcasted_iota(jnp.int32, (UNITS, UNITS // 2), 0)
    col = lax.broadcasted_iota(jnp.int32, (UNITS, UNITS // 2), 1)
    for core, out in ((place.core, mine_ref), (1 - place.core, give_ref)):
        keep = jnp.where(row == (col >> 4) * 32 + core * 16 + (col & 15), 1.0, 0.0).astype(BF16)
        for kind in range(2):
            cols = slice(kind * UNITS, (kind + 1) * UNITS)
            out[:, kind * UNITS // 2 : (kind + 1) * UNITS // 2] = mm(both_ref[:, cols], keep).astype(BF16)


def slope_kernel(first_row, count_ref, own_ref, r1, r2, r3, cot_ref, grad_ref):
    pre = own_ref[...] + r1[...].astype(F32) + r2[...].astype(F32) + r3[...].astype(F32)
    sig = 1.0 / (1.0 + jnp.exp(-pre))
    slope = cot_ref[first_row : first_row + ROWS // 2, :].astype(F32) * (sig * (1.0 + pre * (1.0 - sig)))
    live = lax.broadcasted_iota(jnp.int32, pre.shape, 0) + first_row < count_ref[0]
    grad_ref[...] = jnp.where(live, slope, 0.0).astype(BF16)


def spread_kernel(
    place, g0a, g0b, g1a, g1b, g2a, g2b, g3a, g3b, w_ref, inv_ref, adjt_ref, halo_ref, own_hbm, others_ref,
    own_ref, sems,
):
    parts = ((g0a, g0b), (g1a, g1b), (g2a, g2b), (g3a, g3b))
    rows = ROWS // 2
    copies = [
        pltpu.make_async_copy(ref, others_ref.at[d, pl.ds(half * rows, rows)], sems.at[2 * d + half])
        for d, pair in enumerate(parts)
        for half, ref in enumerate(pair)
    ]
    for copy in copies:
        copy.start()
    grads = {d: jnp.concatenate([upper[...], lower[...]], axis=0) for d, (upper, lower) in enumerate(parts)}

    def back(base):
        total = None
        for d in (0, 3, 1, 2):
            origin = lax.rem(place.hid + HID - d, HID)
            cols = pl.ds(pl.multiple_of(origin * UNITS, UNITS), UNITS)
            term = mm_last(grads[d], w_ref[base : base + UNITS, cols])
            total = term if total is None else total + term
        return total

    mean = (back(UNITS) * wide(inv_ref[...], UNITS)).astype(BF16)
    own_ref[...] = back(0) + mm(adjt_ref[:ROWS, :], mean)
    copies.append(pltpu.make_async_copy(own_ref, own_hbm, sems.at[8]))
    copies[-1].start()
    halo_ref[...] = mm(adjt_ref[ROWS:, :], mean).astype(BF16).reshape(PEERS, SLOTS, UNITS)
    for copy in copies:
        copy.wait()


def outer_second_kernel(slots, place, grads_hbm, mates_ref, stacked_hbm, mate_ref, *refs):
    outs, (block_ref, grads_ref, mine_ref, load_sems, sems) = refs[:4], refs[4:]
    loads = [pltpu.make_async_copy(grads_hbm.at[0], grads_ref.at[0], load_sems.at[0])]
    for source, target, base in ((stacked_hbm, mine_ref, 4),):
        for piece in range(2):
            rows = pl.ds(piece * ROWS // 2, ROWS // 2)
            loads.append(pltpu.make_async_copy(source.at[rows], target.at[rows], load_sems.at[base + piece]))
    loads += [
        pltpu.make_async_copy(grads_hbm.at[index], grads_ref.at[index], load_sems.at[index]) for index in (1, 2, 3)
    ]
    for load in loads:
        load.start()
    row = lax.broadcasted_iota(jnp.int32, (UNITS, UNITS // 2), 0)
    col = lax.broadcasted_iota(jnp.int32, (UNITS, UNITS // 2), 1)
    wanted = (col >> 6) * 128 + place.core * 64 + (col & 63)
    keep = jnp.where(row == wanted, 1.0, 0.0).astype(BF16)
    for index, slot in enumerate(slots):
        other = mm(mates_ref[index], keep).astype(BF16)
        loads[index + 2 if index else 0].wait()
        mine = mm(grads_ref[index], keep).astype(BF16)
        if index == 0:
            for load in loads[1:3]:
                load.wait()
        total = mm_first(mine, mine_ref[...]) + mm_first(other, mate_ref[...])
        block_ref[index] = total.astype(BF16).reshape(HID, 64, 2 * UNITS)

        @pl.when(place.core == 0)
        def _():
            for d, out in enumerate(outs):
                source = block_ref.at[index, lax.rem(place.z + d, HID)]
                pltpu.make_async_copy(source, out.at[slot], sems.at[index, d]).start()

        step = lax.rem(place.hid + 2 * HID - place.x - slot, HID)
        for d, out in enumerate(outs):

            @pl.when((place.core == 1) & (step == d))
            def _():
                for z in range(HID):
                    pltpu.make_async_copy(block_ref.at[index, z], out.at[z], sems.at[index, z]).start()

    for index, slot in enumerate(slots):
        for d, out in enumerate(outs):
            pltpu.make_async_copy(block_ref.at[index, d], out.at[slot], sems.at[index, d]).wait()


def along_kernel(place, z0, z1, z2, z3, x0, x1, x2, x3):
    for d, out in enumerate((x0, x1, x2, x3)):
        by_x = lax.rem(place.hid + 2 * HID - place.x - d, HID)
        at = jnp.where(place.core == 0, by_x, lax.rem(place.z + d, HID))
        total = z0[at].astype(F32) + z1[at].astype(F32) + z2[at].astype(F32) + z3[at].astype(F32)
        out[...] = total.astype(out.dtype)


def last_second_kernel(scale, x0, x1, x2, x3, out_ref):
    total = x0[...] + x1[...].astype(F32) + x2[...].astype(F32) + x3[...].astype(F32)
    total = total * scale
    out_ref[:, 0, :] = total[:, :UNITS]
    out_ref[:, 1, :] = total[:, UNITS:]


def settle_kernel(
    place, back_ref, own_ref, slope_ref, selt_ref, w_ref, grad_ref, mine_ref, s1, s2, s3, full_ref
):
    me = place.hid
    grad = own_ref[...] + mm(selt_ref[...], back_ref[...].reshape(FAR, UNITS))
    grad = (grad * slope_ref[...]).astype(BF16)
    grad_ref[...] = grad
    full_ref[...] = mm_last(grad, w_ref[...])
    for d, out in ((2, s2), (1, s1), (3, s3), (0, mine_ref)):
        target = lax.rem(me + d, HID)
        for half, base in ((1, 0), (0, UNITS)):
            cols = pl.ds(pl.multiple_of(base + target * LANES, LANES), LANES)
            out[:, half * LANES : (half + 1) * LANES] = full_ref[:, cols].astype(out.dtype)


def outer_first_kernel(grad_ref, grad_mate_ref, mine_ref, mate_ref, out_ref):
    product = mm_first(mine_ref[...], grad_ref[...]) + mm_first(mate_ref[...], grad_mate_ref[...])
    product = product.astype(BF16).reshape(2, CHIPS, SLOTS, UNITS)
    for part in range(HID):
        for kind in range(2):
            start = (part * 2 + kind) * SLOTS
            out_ref[:, start : start + SLOTS] = product[kind, :, :, part * LANES : (part + 1) * LANES]


def return_kernel(mine_ref, r1, r2, r3, inv_ref, adjt_ref, merged_ref, base_ref, out_ref, halo_ref, sem):
    total = mine_ref[...] + r1[...].astype(F32) + r2[...].astype(F32) + r3[...].astype(F32)
    mean = (total[:, :LANES] * inv_ref[...]).astype(BF16)
    halo_ref[...] = mm(adjt_ref[ROWS:, :], mean).astype(BF16).reshape(CHIPS, 2 * SLOTS, LANES)
    copy = pltpu.make_async_copy(halo_ref, out_ref.at[:, pl.ds(LANES, 2 * SLOTS), :], sem)
    copy.start()
    base_ref[...] = total[:, LANES:] + mm(adjt_ref[:ROWS, :], mean)
    copy.wait()


def hand_kernel(place, parts_ref, mine_ref, give_ref):
    for core, out in ((place.core, mine_ref), (1 - place.core, give_ref)):
        out[...] = parts_ref[:, pl.ds(pl.multiple_of(LANES + core * SLOTS, SLOTS), SLOTS), :]


def weights_kernel(scale, parts_ref, weight_ref):
    total = parts_ref[0, :LANES].astype(F32)
    for index in range(1, CHIPS):
        total = total + parts_ref[index, :LANES].astype(F32)
    for part in range(HID):
        for kind in range(2):
            start = (part * 2 + kind) * SLOTS
            weight_ref[:, kind, part * LANES : (part + 1) * LANES] = total[start : start + SLOTS] * scale


def final_kernel(place, base_ref, selt_ref, mine_ref, mate_ref, feat_ref, back_ref):
    back_ref[:, place.core] = mine_ref[...]
    back_ref[:, 1 - place.core] = mate_ref[...]
    feat_ref[...] = base_ref[...] + mm(selt_ref[...], back_ref[...].reshape(FAR, LANES))


class Place:
    def __init__(self):
        node = lax.axis_index("nodes")
        self.hid = lax.axis_index("hid")
        self.core = node & 1
        self.x = node >> 3
        self.z = (node >> 1) & 3


class Late:
    def __init__(self, source, ref, sem):
        self.ref = ref
        self.source = source
        self.copy = pltpu.make_async_copy(source, ref, sem)
        self.copy.start()
        self.waited = False

    def __getitem__(self, index):
        if not self.waited:
            self.copy.wait()
            self.waited = True
        return self.ref[index]


def in_hbm(value):
    return pltpu.with_memory_space_constraint(value, pltpu.HBM)


def call(
    kernel, name, operands, outs, scratch=(), placed=False, scalars=0, after=(), late=(), held=(), stored=(),
    loose=(), pinned=(), aliases=None, work=1,
):
    shapes = [jax.ShapeDtypeStruct(shape, dtype) for shape, dtype in outs]
    for index in (*stored, *loose):
        shapes[index] = pltpu.HBM(*outs[index])
    for index in pinned:
        shapes[index] = pltpu.VMEM(*outs[index])
    operands = [in_hbm(o) if index in (*late, *held) else o for index, o in enumerate(operands)]
    count = len(operands)
    in_specs = [
        pl.BlockSpec(memory_space=pltpu.SMEM if index < scalars else pltpu.VMEM) for index in range(count)
    ] + [pl.BlockSpec(memory_space=pl.ANY)] * len(after)
    for index in (*late, *held, *(aliases or {})):
        in_specs[index] = pl.BlockSpec(memory_space=pltpu.HBM)
    out_specs = [
        pl.BlockSpec(memory_space=pltpu.HBM if index in (*stored, *loose) else pltpu.VMEM)
        for index in range(len(shapes))
    ]
    first_out = count + len(after)
    fixed = first_out + len(shapes) + len(scratch)
    buffers = [pltpu.VMEM(operands[index].shape, operands[index].dtype) for index in late]
    buffers += [pltpu.VMEM(*outs[index]) for index in stored]
    sems = [pltpu.SemaphoreType.DMA for _ in buffers]

    def body(*refs):
        inputs = list(refs[:count])
        outputs = list(refs[first_out : first_out + len(shapes)])
        spare, flags = refs[fixed : fixed + len(buffers)], refs[fixed + len(buffers) :]
        for slot, index in enumerate(late):
            inputs[index] = Late(inputs[index], spare[slot], flags[slot])
        copies = []
        for slot, index in enumerate(stored, len(late)):
            copies.append(pltpu.make_async_copy(spare[slot], outputs[index], flags[slot]))
            outputs[index] = spare[slot]
        kernel(*([Place()] if placed else []), *inputs, *outputs, *refs[first_out + len(shapes) : fixed])
        for copy in copies:
            copy.start()
        for copy in copies:
            copy.wait()

    moved = sum(o.size * o.dtype.itemsize for o in operands) + sum(
        math.prod(shape) * jnp.dtype(dtype).itemsize for shape, dtype in outs
    )
    results = pl.pallas_call(
        body,
        out_shape=shapes,
        in_specs=in_specs,
        out_specs=out_specs,
        scratch_shapes=list(scratch) + buffers + sems,
        input_output_aliases=aliases or {},
        compiler_params=pltpu.CompilerParams(vmem_limit_bytes=16 * 1024 * 1024),
        cost_estimate=pl.CostEstimate(flops=work * BIG, bytes_accessed=moved, transcendentals=0),
        name=name,
    )(*operands, *after)
    return results[0] if len(outs) == 1 else results


def around(values):
    return [lax.ppermute(v, "hid", [(i, (i + d) % HID) for i in range(HID)]) for d, v in values]


def node_at(x, z, core):
    return ((x % 4) * 4 + z % 4) * 2 + core


def swap(value):
    return lax.ppermute(value, "nodes", [(i, i ^ 1) for i in range(PEERS)])


def near(values, turned):
    def target(x, z, core, d):
        return node_at(x, z + d, core) if (core == 0) != turned else node_at(x + d, z, core)

    return [
        lax.ppermute(v, "nodes", [
            (node_at(x, z, c), target(x, z, c, d)) for x in range(4) for z in range(4) for c in range(2)
        ])
        for d, v in values
    ]


def on_device(features, neighbors, degree, send_rows, node_count, w_first, w_second, cotangent):
    scale = float(ROWS * PEERS) ** (-0.5)
    routes = jnp.swapaxes(send_rows, 1, 2).reshape(SLOTS, PEERS)
    w1 = w_first.reshape(2 * UNITS, UNITS)
    w2 = w_second.reshape(2 * UNITS, HID * UNITS)
    chunk = ((ROWS, UNITS), BF16)

    wide_chunk = ((ROWS, UNITS), F32)
    halo = ((PEERS, SLOTS, UNITS), BF16)
    sel, send_feat = call(
        pick_kernel, "pick", (routes, features),
        [((FAR, ROWS), BF16), ((PEERS, HID, SLOTS, LANES), BF16)], late=(0, 1), work=1,
    )
    far_feat = lax.all_to_all(
        send_feat.reshape(PEERS * HID, SLOTS, LANES), ("nodes", "hid"), 0, 0, tiled=True
    ).reshape(PEERS, HID, SLOTS, LANES)
    f2, f1, f3 = around([(2, features), (1, features), (3, features)])
    adj, adjt, inv = call(
        count_kernel, "count", (jnp.swapaxes(neighbors, 0, 1), degree.reshape(1, ROWS)),
        [((ROWS, ROWS + FAR), BF16), ((ROWS + FAR, ROWS), BF16), ((ROWS, LANES), F32)],
        scratch=[pltpu.VMEM((KEPT, ROWS), jnp.int32)] * 3, late=(1, 0), work=8, after=(sel,),
    )
    both, hidden, send_hidden = call(
        first_kernel, "first", (features, f1, f2, f3, far_feat, adj, inv, w1, sel),
        [((ROWS, 2 * UNITS), BF16), chunk, halo], work=6, placed=True,
        scratch=[pltpu.VMEM((FAR, UNITS), BF16)],
    )
    far_hidden = lax.all_to_all(send_hidden, "nodes", 0, 0, tiled=True)
    half_chunk = ((ROWS // 2, UNITS), BF16)
    stacked, own_a, own_b, s1a, s1b, s2a, s2b, s3a, s3b = call(
        second_kernel, "second", (hidden, far_hidden, adj, inv, w2),
        [((ROWS, 2 * UNITS), BF16)] + [((ROWS // 2, UNITS), F32)] * 2 + [half_chunk] * 6,
        scratch=[pltpu.VMEM((HID, 2 * UNITS, UNITS), BF16), pltpu.SemaphoreType.DMA((HID, 4))],
        placed=True, work=10, held=(4,),
    )
    r2a, r1a, r3a = around([(2, s2a), (1, s1a), (3, s3a)])
    r2b, r1b, r3b = around([(2, s2b), (1, s1b), (3, s3b)])
    slope, saved, selt = call(
        gate_kernel, "gate", (both, stacked, w1, routes),
        [wide_chunk, ((ROWS, 2 * UNITS), BF16), ((ROWS, FAR), BF16)],
        after=(s1a,), late=(2, 3), stored=(0, 1, 2), work=2,
    )
    saved_mate = swap(saved)
    def gradient(first_row, own, parts):
        return call(
            lambda *refs: slope_kernel(first_row, *refs), "slope", (node_count, own, *parts, cotangent),
            [half_chunk], scalars=1, after=(in_hbm(slope),),
        )

    g0a = gradient(0, own_a, (r1a, r2a, r3a))
    g2a, g1a, g3a = around([(2, g0a), (1, g0a), (3, g0a)])
    g0b = gradient(ROWS // 2, own_b, (r1b, r2b, r3b))
    g2b, g1b, g3b = around([(2, g0b), (1, g0b), (3, g0b)])

    mine_rows, give_rows = call(
        choose_kernel, "choose", (both,), [chunk, chunk], placed=True, stored=(0, 1), work=4, after=(g0b,),
    )
    mate_rows = swap(give_rows)
    halo_hidden, own_hidden, others = call(
        spread_kernel, "spread", (g0a, g0b, g1a, g1b, g2a, g2b, g3a, g3b, w2, inv, adjt),
        [halo, wide_chunk, ((HID, ROWS, UNITS), BF16)], placed=True, work=10, loose=(1, 2), after=(in_hbm(mine_rows),),
        scratch=[pltpu.VMEM((ROWS, UNITS), F32), pltpu.SemaphoreType.DMA((9,))],
    )
    back_hidden = lax.all_to_all(halo_hidden, "nodes", 0, 0, tiled=True)
    slots = (0, 1, 2, 3)
    z0, z1, z2, z3 = call(
        lambda *refs: outer_second_kernel(slots, *refs), "outer_second",
        (others, swap(others), saved, saved_mate), [((HID, 64, 2 * UNITS), BF16)] * HID,
        scratch=[
            pltpu.VMEM((HID, HID, 64, 2 * UNITS), BF16), pltpu.VMEM((HID, ROWS, UNITS), BF16),
            pltpu.VMEM((ROWS, 2 * UNITS), BF16), pltpu.SemaphoreType.DMA((8,)),
            pltpu.SemaphoreType.DMA((HID, HID)),
        ],
        placed=True, loose=slots, held=(0, 2), work=12,
    )
    outer_done = in_hbm(z0)
    z2, z1, z3 = near([(2, z2), (1, z1), (3, z3)], False)
    grad, mine, s1, s2, s3 = call(
        settle_kernel, "settle",
        (back_hidden, own_hidden, slope, selt, w1),
        [chunk, ((ROWS, 2 * LANES), F32)] + [((ROWS, 2 * LANES), BF16)] * 3,
        scratch=[pltpu.VMEM((ROWS, 2 * UNITS), F32)], placed=True, late=(3, 1, 2, 4), work=6, after=(outer_done,),
    )
    r2, r1, r3 = around([(2, s2), (1, s1), (3, s3)])
    merged = call(
        outer_first_kernel, "outer_first", (grad, swap(grad), mine_rows, mate_rows),
        [((CHIPS, LANES + 2 * SLOTS, LANES), BF16)], after=(s1,), late=(2,), stored=(0,), work=2,
    )
    x0, x1, x2, x3 = call(
        along_kernel, "along", (z0, z1, z2, z3),
        [((64, 2 * UNITS), F32)] + [((64, 2 * UNITS), BF16)] * 3, placed=True, late=(0,), after=(s1,),
    )
    base, merged = call(
        return_kernel, "return", (mine, r1, r2, r3, inv, adjt, merged),
        [((ROWS, LANES), F32), ((CHIPS, LANES + 2 * SLOTS, LANES), BF16)],
        scratch=[pltpu.VMEM((CHIPS, 2 * SLOTS, LANES), BF16), pltpu.SemaphoreType.DMA],
        loose=(1,), aliases={6: 1}, after=(x0,),
    )
    same_core = [[2 * chip + core for chip in range(CHIPS)] for core in range(2)]
    parts = lax.all_to_all(merged, "nodes", 0, 0, tiled=True, axis_index_groups=same_core)
    block = ((CHIPS, SLOTS, LANES), BF16)
    mine_back, give_back = call(hand_kernel, "hand", (parts,), [block, block], placed=True)
    mate_back = swap(give_back)
    x2, x1, x3 = near([(2, x2), (1, x1), (3, x3)], True)
    grad_w_first = call(
        lambda *refs: weights_kernel(scale, *refs), "weights", (parts,), [((SLOTS, 2, UNITS), F32)],
        after=(give_back,),
    )
    grad_features = call(
        final_kernel, "final", (base, selt, mine_back, mate_back), [((ROWS, LANES), F32)],
        placed=True, scratch=[pltpu.VMEM((CHIPS, 2, SLOTS, LANES), BF16)],
    )
    grad_w_second = call(
        lambda *refs: last_second_kernel(scale, *refs), "last_second", (x0, x1, x2, x3), [((64, 2, UNITS), F32)],
    )
    return grad_w_first, grad_w_second, grad_features


def solution(mesh):
    placed = (
        P("nodes", "hid"),
        P("nodes", None),
        P("nodes"),
        P("nodes", None, None),
        P("nodes"),
        P(None, None, "hid"),
        P(None, "hid", None),
        P("nodes", "hid"),
    )
    return jax.shard_map(
        on_device,
        mesh=mesh,
        in_specs=placed,
        out_specs=(P("nodes", None, "hid"), P("nodes", None, "hid"), P("nodes", "hid")),
        check_vma=False,
    )
```

```python
import math

import jax
import jax.numpy as jnp
from jax import lax
from jax.experimental import pallas as pl
from jax.experimental.pallas import tpu as pltpu
from jax.sharding import PartitionSpec as P

BF16 = jnp.bfloat16
F32 = jnp.float32
ROWS = 256
PEERS = 32
SLOTS = 16
FAR = PEERS * SLOTS
HID = 4
LANES = 128
UNITS = 512
KEPT = 80
CHIPS = 16
BIG = 2 * ROWS * UNITS * UNITS


def mm(left_op, right_op):
    return jnp.dot(left_op, right_op, preferred_element_type=F32)


def mm_last(left_op, right_op):
    return lax.dot_general(left_op, right_op, (((1,), (1,)), ((), ())), preferred_element_type=F32)


def mm_first(left_op, right_op):
    return lax.dot_general(left_op, right_op, (((0,), (0,)), ((), ())), preferred_element_type=F32)


def wide(column, width):
    return jnp.concatenate([column] * (width // LANES), axis=1)


def route_rows(routes_ref):
    peer = lax.broadcasted_iota(jnp.int32, (PEERS, FAR), 0)
    lane_peer = lax.broadcasted_iota(jnp.int32, (PEERS, FAR), 1) >> 4
    spread_out = jnp.where(peer == lane_peer, 1.0, 0.0).astype(BF16)
    by_slot = mm(routes_ref[...].astype(F32).astype(BF16), spread_out)
    slot = lax.broadcasted_iota(jnp.int32, (SLOTS, FAR), 0)
    lane_slot = lax.broadcasted_iota(jnp.int32, (SLOTS, FAR), 1) & (SLOTS - 1)
    routes = jnp.sum(jnp.where(slot == lane_slot, by_slot, 0.0), axis=0, keepdims=True)
    row = lax.broadcasted_iota(jnp.int32, (ROWS, FAR), 0).astype(F32)
    return jnp.where(row == routes, 1.0, 0.0)


def pick_kernel(routes_ref, feat_ref, sel_ref, send_ref):
    row_peer = lax.broadcasted_iota(jnp.int32, (FAR, PEERS), 0) >> 4
    peer = lax.broadcasted_iota(jnp.int32, (FAR, PEERS), 1)
    by_slot = mm_last(jnp.where(row_peer == peer, 1.0, 0.0).astype(BF16), routes_ref[...].astype(F32).astype(BF16))
    row_slot = lax.broadcasted_iota(jnp.int32, (FAR, SLOTS), 0) & (SLOTS - 1)
    slot = lax.broadcasted_iota(jnp.int32, (FAR, SLOTS), 1)
    routes = jnp.sum(jnp.where(row_slot == slot, by_slot, 0.0), axis=1, keepdims=True)
    row = lax.broadcasted_iota(jnp.int32, (FAR, ROWS), 1).astype(F32)
    sel = jnp.where(row == routes, 1.0, 0.0).astype(BF16)
    sel_ref[...] = sel
    picked = mm(sel, feat_ref[...]).astype(BF16).reshape(PEERS, SLOTS, LANES)
    for part in range(HID):
        send_ref[:, part] = picked


def count_kernel(
    neigh_ref, degree_ref, adj_ref, adjt_ref, inv_ref, key_ref, low_ref, high_ref
):
    inv_ref[...] = 1.0 / jnp.broadcast_to(degree_ref[...].astype(F32), (LANES, ROWS)).T
    entry = neigh_ref[...]
    used = lax.broadcasted_iota(jnp.int32, (KEPT, ROWS), 0) < degree_ref[...]
    block = entry >> 7
    upper = block >= 3
    weight = jnp.where(used, jnp.left_shift(1, 10 * jnp.where(upper, block - 3, block)), 0)
    key_ref[...] = entry & (LANES - 1)
    low_ref[...] = jnp.where(upper, 0, weight)
    high_ref[...] = jnp.where(upper, weight, 0)
    tall = 64
    for half in range(LANES // tall):
        value = lax.broadcasted_iota(jnp.int32, (tall, LANES), 0) + half * tall
        for side in range(ROWS // LANES):
            cols = slice(side * LANES, (side + 1) * LANES)

            def step(index, carry):
                low, high = carry
                at = pl.ds(pl.multiple_of(index * 8, 8), 8)
                keys, lows, highs = key_ref[at, cols], low_ref[at, cols], high_ref[at, cols]
                for j in range(8):
                    same = keys[j : j + 1] == value
                    low = low + jnp.where(same, lows[j : j + 1], 0)
                    high = high + jnp.where(same, highs[j : j + 1], 0)
                return low, high

            empty = jnp.zeros((tall, LANES), jnp.int32)
            low, high = lax.fori_loop(0, KEPT // 8, step, (empty, empty))
            for t in range(3):
                for base, packed in ((0, low), (3, high)):
                    count = jnp.right_shift(packed, 10 * t) & 1023
                    start = (base + t) * LANES + half * tall
                    adjt_ref[start : start + tall, cols] = count.astype(F32).astype(BF16)
    for t in range((ROWS + FAR) // LANES):
        rows = slice(t * LANES, (t + 1) * LANES)
        adj_ref[:, rows] = adjt_ref[rows, :].astype(F32).T.astype(BF16)


def first_kernel(
    place, f0, f1, f2, f3, far_ref, adj_ref, inv_ref, w_ref, sel_ref, both_ref, hidden_ref, send_ref, far_all
):
    for d, piece in enumerate((f0, f1, f2, f3)):
        origin = lax.rem(place.hid + HID - d, HID)
        both_ref[:, pl.ds(pl.multiple_of(origin * LANES, LANES), LANES)] = piece[...]
    for origin in range(HID):
        far_all[:, origin * LANES : (origin + 1) * LANES] = far_ref[:, origin].reshape(FAR, LANES)
    agg = mm(adj_ref[:, :ROWS], both_ref[:, :UNITS]) + mm(adj_ref[:, ROWS:], far_all[...])
    both_ref[:, UNITS:] = (agg * wide(inv_ref[...], UNITS)).astype(BF16)
    pre = mm(both_ref[...], w_ref[...])
    sig = 1.0 / (1.0 + jnp.exp(-pre))
    hidden = (pre * sig).astype(BF16)
    hidden_ref[...] = hidden
    send_ref[...] = mm(sel_ref[...], hidden).astype(BF16).reshape(PEERS, SLOTS, UNITS)


def gate_kernel(both_ref, stacked_ref, w1_ref, routes_ref, slope_ref, saved_ref, selt_ref):
    selt_ref[...] = route_rows(routes_ref).astype(BF16)
    saved_ref[...] = stacked_ref[...]
    pre = mm(both_ref[...], w1_ref[...])
    sig = 1.0 / (1.0 + jnp.exp(-pre))
    slope_ref[...] = sig * (1.0 + pre * (1.0 - sig))


def second_kernel(
    place, hidden_ref, far_ref, adj_ref, inv_ref, w_ref, stacked_ref, own_a, own_b, s1a, s1b, s2a, s2b, s3a, s3b
):
    hidden = hidden_ref[...]
    total = mm(adj_ref[:, :ROWS], hidden) + mm(adj_ref[:, ROWS:], far_ref[...].reshape(FAR, UNITS))
    stacked_ref[:, :UNITS] = hidden
    stacked_ref[:, UNITS:] = (total * wide(inv_ref[...], UNITS)).astype(BF16)
    for d, upper, lower in ((2, s2a, s2b), (1, s1a, s1b), (3, s3a, s3b), (0, own_a, own_b)):
        target = lax.rem(place.hid + d, HID)
        cols = pl.ds(pl.multiple_of(target * UNITS, UNITS), UNITS)
        part = mm(stacked_ref[...], w_ref[:, cols]).astype(upper.dtype)
        upper[...] = part[: ROWS // 2]
        lower[...] = part[ROWS // 2 :]


def choose_kernel(place, both_ref, mine_ref, give_ref):
    row = lax.broadcasted_iota(jnp.int32, (UNITS, UNITS // 2), 0)
    col = lax.broadcasted_iota(jnp.int32, (UNITS, UNITS // 2), 1)
    for core, out in ((place.core, mine_ref), (1 - place.core, give_ref)):
        keep = jnp.where(row == (col >> 4) * 32 + core * 16 + (col & 15), 1.0, 0.0).astype(BF16)
        for kind in range(2):
            cols = slice(kind * UNITS, (kind + 1) * UNITS)
            out[:, kind * UNITS // 2 : (kind + 1) * UNITS // 2] = mm(both_ref[:, cols], keep).astype(BF16)


def slope_kernel(first_row, count_ref, own_ref, r1, r2, r3, cot_ref, grad_ref):
    pre = own_ref[...] + r1[...].astype(F32) + r2[...].astype(F32) + r3[...].astype(F32)
    sig = 1.0 / (1.0 + jnp.exp(-pre))
    slope = cot_ref[first_row : first_row + ROWS // 2, :].astype(F32) * (sig * (1.0 + pre * (1.0 - sig)))
    live = lax.broadcasted_iota(jnp.int32, pre.shape, 0) + first_row < count_ref[0]
    grad_ref[...] = jnp.where(live, slope, 0.0).astype(BF16)


def spread_kernel(
    place, g0a, g0b, g1a, g1b, g2a, g2b, g3a, g3b, w_ref, inv_ref, adjt_ref, halo_ref, own_hbm, others_ref,
    own_ref, sems,
):
    parts = ((g0a, g0b), (g1a, g1b), (g2a, g2b), (g3a, g3b))
    rows = ROWS // 2
    copies = [
        pltpu.make_async_copy(ref, others_ref.at[d, pl.ds(half * rows, rows)], sems.at[2 * d + half])
        for d, pair in enumerate(parts)
        for half, ref in enumerate(pair)
    ]
    for copy in copies:
        copy.start()
    grads = {d: jnp.concatenate([upper[...], lower[...]], axis=0) for d, (upper, lower) in enumerate(parts)}

    def back(base):
        total = None
        for d in (0, 3, 1, 2):
            origin = lax.rem(place.hid + HID - d, HID)
            cols = pl.ds(pl.multiple_of(origin * UNITS, UNITS), UNITS)
            term = mm_last(grads[d], w_ref[base : base + UNITS, cols])
            total = term if total is None else total + term
        return total

    mean = (back(UNITS) * wide(inv_ref[...], UNITS)).astype(BF16)
    own_ref[...] = back(0) + mm(adjt_ref[:ROWS, :], mean)
    copies.append(pltpu.make_async_copy(own_ref, own_hbm, sems.at[8]))
    copies[-1].start()
    halo_ref[...] = mm(adjt_ref[ROWS:, :], mean).astype(BF16).reshape(PEERS, SLOTS, UNITS)
    for copy in copies:
        copy.wait()


def outer_second_kernel(slots, place, grads_hbm, mates_ref, stacked_hbm, mate_ref, *refs):
    outs, (block_ref, grads_ref, mine_ref, load_sems, sems) = refs[:4], refs[4:]
    loads = [pltpu.make_async_copy(grads_hbm.at[0], grads_ref.at[0], load_sems.at[0])]
    for source, target, base in ((stacked_hbm, mine_ref, 4),):
        for piece in range(2):
            rows = pl.ds(piece * ROWS // 2, ROWS // 2)
            loads.append(pltpu.make_async_copy(source.at[rows], target.at[rows], load_sems.at[base + piece]))
    loads += [
        pltpu.make_async_copy(grads_hbm.at[index], grads_ref.at[index], load_sems.at[index]) for index in (1, 2, 3)
    ]
    for load in loads:
        load.start()
    row = lax.broadcasted_iota(jnp.int32, (UNITS, UNITS // 2), 0)
    col = lax.broadcasted_iota(jnp.int32, (UNITS, UNITS // 2), 1)
    wanted = (col >> 6) * 128 + place.core * 64 + (col & 63)
    keep = jnp.where(row == wanted, 1.0, 0.0).astype(BF16)
    for index, slot in enumerate(slots):
        other = mm(mates_ref[index], keep).astype(BF16)
        loads[index + 2 if index else 0].wait()
        mine = mm(grads_ref[index], keep).astype(BF16)
        if index == 0:
            for load in loads[1:3]:
                load.wait()
        total = mm_first(mine, mine_ref[...]) + mm_first(other, mate_ref[...])
        block_ref[index] = total.astype(BF16).reshape(HID, 64, 2 * UNITS)

        @pl.when(place.core == 0)
        def _():
            for d, out in enumerate(outs):
                source = block_ref.at[index, lax.rem(place.z + d, HID)]
                pltpu.make_async_copy(source, out.at[slot], sems.at[index, d]).start()

        step = lax.rem(place.hid + 2 * HID - place.x - slot, HID)
        for d, out in enumerate(outs):

            @pl.when((place.core == 1) & (step == d))
            def _():
                for z in range(HID):
                    pltpu.make_async_copy(block_ref.at[index, z], out.at[z], sems.at[index, z]).start()

    for index, slot in enumerate(slots):
        for d, out in enumerate(outs):
            pltpu.make_async_copy(block_ref.at[index, d], out.at[slot], sems.at[index, d]).wait()


def along_kernel(place, z0, z1, z2, z3, x0, x1, x2, x3):
    for d, out in enumerate((x0, x1, x2, x3)):
        by_x = lax.rem(place.hid + 2 * HID - place.x - d, HID)
        at = jnp.where(place.core == 0, by_x, lax.rem(place.z + d, HID))
        total = z0[at].astype(F32) + z1[at].astype(F32) + z2[at].astype(F32) + z3[at].astype(F32)
        out[...] = total.astype(out.dtype)


def settle_kernel(
    place, back_ref, own_ref, slope_ref, selt_ref, w_ref, grad_ref, mine_ref, s1, s2, s3, full_ref
):
    me = place.hid
    grad = own_ref[...] + mm(selt_ref[...], back_ref[...].reshape(FAR, UNITS))
    grad = (grad * slope_ref[...]).astype(BF16)
    grad_ref[...] = grad
    full_ref[...] = mm_last(grad, w_ref[...])
    for d, out in ((2, s2), (1, s1), (3, s3), (0, mine_ref)):
        target = lax.rem(me + d, HID)
        for half, base in ((1, 0), (0, UNITS)):
            cols = pl.ds(pl.multiple_of(base + target * LANES, LANES), LANES)
            out[:, half * LANES : (half + 1) * LANES] = full_ref[:, cols].astype(out.dtype)


def outer_first_kernel(grad_ref, grad_mate_ref, mine_ref, mate_ref, out_ref):
    product = mm_first(mine_ref[...], grad_ref[...]) + mm_first(mate_ref[...], grad_mate_ref[...])
    product = product.astype(BF16).reshape(2, CHIPS, SLOTS, UNITS)
    for part in range(HID):
        for kind in range(2):
            start = (part * 2 + kind) * SLOTS
            out_ref[:, start : start + SLOTS] = product[kind, :, :, part * LANES : (part + 1) * LANES]


def return_kernel(mine_ref, r1, r2, r3, inv_ref, adjt_ref, merged_ref, base_ref, out_ref, halo_ref, sem):
    total = mine_ref[...] + r1[...].astype(F32) + r2[...].astype(F32) + r3[...].astype(F32)
    mean = (total[:, :LANES] * inv_ref[...]).astype(BF16)
    halo_ref[...] = mm(adjt_ref[ROWS:, :], mean).astype(BF16).reshape(CHIPS, 2 * SLOTS, LANES)
    copy = pltpu.make_async_copy(halo_ref, out_ref.at[:, pl.ds(LANES, 2 * SLOTS), :], sem)
    copy.start()
    base_ref[...] = total[:, LANES:] + mm(adjt_ref[:ROWS, :], mean)
    copy.wait()


def hand_kernel(place, parts_ref, mine_ref, give_ref):
    for core, out in ((place.core, mine_ref), (1 - place.core, give_ref)):
        out[...] = parts_ref[:, pl.ds(pl.multiple_of(LANES + core * SLOTS, SLOTS), SLOTS), :]


def weights_kernel(scale, x0, x1, x2, x3, parts_ref, second_ref, first_ref):
    total = parts_ref[0, :LANES].astype(F32)
    for index in range(1, CHIPS):
        total = total + parts_ref[index, :LANES].astype(F32)
    total = total * scale
    for part in range(HID):
        for kind in range(2):
            start = (part * 2 + kind) * SLOTS
            first_ref[:, kind, part * LANES : (part + 1) * LANES] = total[start : start + SLOTS]
    total = (x0[...] + x1[...].astype(F32) + x2[...].astype(F32) + x3[...].astype(F32)) * scale
    second_ref[:, 0, :] = total[:, :UNITS]
    second_ref[:, 1, :] = total[:, UNITS:]


def final_kernel(place, base_ref, selt_ref, mine_ref, mate_ref, feat_ref, back_ref):
    back_ref[:, place.core] = mine_ref[...]
    back_ref[:, 1 - place.core] = mate_ref[...]
    feat_ref[...] = base_ref[...] + mm(selt_ref[...], back_ref[...].reshape(FAR, LANES))


class Place:
    def __init__(self):
        node = lax.axis_index("nodes")
        self.hid = lax.axis_index("hid")
        self.core = node & 1
        self.x = node >> 3
        self.z = (node >> 1) & 3


class Late:
    def __init__(self, source, ref, sem):
        self.ref = ref
        self.source = source
        self.copy = pltpu.make_async_copy(source, ref, sem)
        self.copy.start()
        self.waited = False

    def __getitem__(self, index):
        if not self.waited:
            self.copy.wait()
            self.waited = True
        return self.ref[index]


def in_hbm(value):
    return pltpu.with_memory_space_constraint(value, pltpu.HBM)


def call(
    kernel, name, operands, outs, scratch=(), placed=False, scalars=0, after=(), late=(), held=(), stored=(),
    loose=(), pinned=(), aliases=None, work=1,
):
    shapes = [jax.ShapeDtypeStruct(shape, dtype) for shape, dtype in outs]
    for index in (*stored, *loose):
        shapes[index] = pltpu.HBM(*outs[index])
    for index in pinned:
        shapes[index] = pltpu.VMEM(*outs[index])
    operands = [in_hbm(o) if index in (*late, *held) else o for index, o in enumerate(operands)]
    count = len(operands)
    in_specs = [
        pl.BlockSpec(memory_space=pltpu.SMEM if index < scalars else pltpu.VMEM) for index in range(count)
    ] + [pl.BlockSpec(memory_space=pl.ANY)] * len(after)
    for index in (*late, *held, *(aliases or {})):
        in_specs[index] = pl.BlockSpec(memory_space=pltpu.HBM)
    out_specs = [
        pl.BlockSpec(memory_space=pltpu.HBM if index in (*stored, *loose) else pltpu.VMEM)
        for index in range(len(shapes))
    ]
    first_out = count + len(after)
    fixed = first_out + len(shapes) + len(scratch)
    buffers = [pltpu.VMEM(operands[index].shape, operands[index].dtype) for index in late]
    buffers += [pltpu.VMEM(*outs[index]) for index in stored]
    sems = [pltpu.SemaphoreType.DMA for _ in buffers]

    def body(*refs):
        inputs = list(refs[:count])
        outputs = list(refs[first_out : first_out + len(shapes)])
        spare, flags = refs[fixed : fixed + len(buffers)], refs[fixed + len(buffers) :]
        for slot, index in enumerate(late):
            inputs[index] = Late(inputs[index], spare[slot], flags[slot])
        copies = []
        for slot, index in enumerate(stored, len(late)):
            copies.append(pltpu.make_async_copy(spare[slot], outputs[index], flags[slot]))
            outputs[index] = spare[slot]
        kernel(*([Place()] if placed else []), *inputs, *outputs, *refs[first_out + len(shapes) : fixed])
        for copy in copies:
            copy.start()
        for copy in copies:
            copy.wait()

    moved = sum(o.size * o.dtype.itemsize for o in operands) + sum(
        math.prod(shape) * jnp.dtype(dtype).itemsize for shape, dtype in outs
    )
    results = pl.pallas_call(
        body,
        out_shape=shapes,
        in_specs=in_specs,
        out_specs=out_specs,
        scratch_shapes=list(scratch) + buffers + sems,
        input_output_aliases=aliases or {},
        compiler_params=pltpu.CompilerParams(vmem_limit_bytes=16 * 1024 * 1024),
        cost_estimate=pl.CostEstimate(flops=work * BIG, bytes_accessed=moved, transcendentals=0),
        name=name,
    )(*operands, *after)
    return results[0] if len(outs) == 1 else results


def around(values):
    return [lax.ppermute(v, "hid", [(i, (i + d) % HID) for i in range(HID)]) for d, v in values]


def node_at(x, z, core):
    return ((x % 4) * 4 + z % 4) * 2 + core


def swap(value):
    return lax.ppermute(value, "nodes", [(i, i ^ 1) for i in range(PEERS)])


def near(values, turned):
    def target(x, z, core, d):
        return node_at(x, z + d, core) if (core == 0) != turned else node_at(x + d, z, core)

    return [
        lax.ppermute(v, "nodes", [
            (node_at(x, z, c), target(x, z, c, d)) for x in range(4) for z in range(4) for c in range(2)
        ])
        for d, v in values
    ]


def on_device(features, neighbors, degree, send_rows, node_count, w_first, w_second, cotangent):
    scale = float(ROWS * PEERS) ** (-0.5)
    routes = jnp.swapaxes(send_rows, 1, 2).reshape(SLOTS, PEERS)
    w1 = w_first.reshape(2 * UNITS, UNITS)
    w2 = w_second.reshape(2 * UNITS, HID * UNITS)
    chunk = ((ROWS, UNITS), BF16)

    wide_chunk = ((ROWS, UNITS), F32)
    halo = ((PEERS, SLOTS, UNITS), BF16)
    sel, send_feat = call(
        pick_kernel, "pick", (routes, features),
        [((FAR, ROWS), BF16), ((PEERS, HID, SLOTS, LANES), BF16)], late=(0, 1), work=1,
    )
    far_feat = lax.all_to_all(
        send_feat.reshape(PEERS * HID, SLOTS, LANES), ("nodes", "hid"), 0, 0, tiled=True
    ).reshape(PEERS, HID, SLOTS, LANES)
    f2, f1, f3 = around([(2, features), (1, features), (3, features)])
    adj, adjt, inv = call(
        count_kernel, "count", (jnp.swapaxes(neighbors, 0, 1), degree.reshape(1, ROWS)),
        [((ROWS, ROWS + FAR), BF16), ((ROWS + FAR, ROWS), BF16), ((ROWS, LANES), F32)],
        scratch=[pltpu.VMEM((KEPT, ROWS), jnp.int32)] * 3, late=(1, 0), work=8, after=(sel,),
    )
    both, hidden, send_hidden = call(
        first_kernel, "first", (features, f1, f2, f3, far_feat, adj, inv, w1, sel),
        [((ROWS, 2 * UNITS), BF16), chunk, halo], work=60, placed=True,
        scratch=[pltpu.VMEM((FAR, UNITS), BF16)],
    )
    far_hidden = lax.all_to_all(send_hidden, "nodes", 0, 0, tiled=True)
    half_chunk = ((ROWS // 2, UNITS), BF16)
    stacked, own_a, own_b, s1a, s1b, s2a, s2b, s3a, s3b = call(
        second_kernel, "second", (hidden, far_hidden, adj, inv, w2),
        [((ROWS, 2 * UNITS), BF16)] + [((ROWS // 2, UNITS), F32)] * 2 + [half_chunk] * 6,
        placed=True, work=10,
    )
    r2a, r1a, r3a = around([(2, s2a), (1, s1a), (3, s3a)])
    r2b, r1b, r3b = around([(2, s2b), (1, s1b), (3, s3b)])
    slope, saved, selt = call(
        gate_kernel, "gate", (both, stacked, w1, routes),
        [wide_chunk, ((ROWS, 2 * UNITS), BF16), ((ROWS, FAR), BF16)],
        after=(s1a,), late=(2, 3), stored=(0, 1, 2), work=2,
    )
    saved_mate = swap(saved)
    def gradient(first_row, own, parts):
        return call(
            lambda *refs: slope_kernel(first_row, *refs), "slope", (node_count, own, *parts, cotangent),
            [half_chunk], scalars=1, after=(in_hbm(slope),),
        )

    g0a = gradient(0, own_a, (r1a, r2a, r3a))
    g2a, g1a, g3a = around([(2, g0a), (1, g0a), (3, g0a)])
    g0b = gradient(ROWS // 2, own_b, (r1b, r2b, r3b))
    g2b, g1b, g3b = around([(2, g0b), (1, g0b), (3, g0b)])

    mine_rows, give_rows = call(
        choose_kernel, "choose", (both,), [chunk, chunk], placed=True, stored=(0, 1), work=4, after=(g0b,),
    )
    mate_rows = swap(give_rows)
    halo_hidden, own_hidden, others = call(
        spread_kernel, "spread", (g0a, g0b, g1a, g1b, g2a, g2b, g3a, g3b, w2, inv, adjt),
        [halo, wide_chunk, ((HID, ROWS, UNITS), BF16)], placed=True, work=10, loose=(1, 2), after=(in_hbm(mine_rows),),
        scratch=[pltpu.VMEM((ROWS, UNITS), F32), pltpu.SemaphoreType.DMA((9,))],
    )
    back_hidden = lax.all_to_all(halo_hidden, "nodes", 0, 0, tiled=True)
    slots = (0, 1, 2, 3)
    z0, z1, z2, z3 = call(
        lambda *refs: outer_second_kernel(slots, *refs), "outer_second",
        (others, swap(others), saved, saved_mate), [((HID, 64, 2 * UNITS), BF16)] * HID,
        scratch=[
            pltpu.VMEM((HID, HID, 64, 2 * UNITS), BF16), pltpu.VMEM((HID, ROWS, UNITS), BF16),
            pltpu.VMEM((ROWS, 2 * UNITS), BF16), pltpu.SemaphoreType.DMA((8,)),
            pltpu.SemaphoreType.DMA((HID, HID)),
        ],
        placed=True, loose=slots, held=(0, 2), work=12,
    )
    outer_done = in_hbm(z0)
    z2, z1, z3 = near([(2, z2), (1, z1), (3, z3)], False)
    grad, mine, s1, s2, s3 = call(
        settle_kernel, "settle",
        (back_hidden, own_hidden, slope, selt, w1),
        [chunk, ((ROWS, 2 * LANES), F32)] + [((ROWS, 2 * LANES), BF16)] * 3,
        scratch=[pltpu.VMEM((ROWS, 2 * UNITS), F32)], placed=True, late=(3, 1, 2, 4), work=6, after=(outer_done,),
    )
    r2, r1, r3 = around([(2, s2), (1, s1), (3, s3)])
    merged = call(
        outer_first_kernel, "outer_first", (grad, swap(grad), mine_rows, mate_rows),
        [((CHIPS, LANES + 2 * SLOTS, LANES), BF16)], after=(s1,), late=(2,), stored=(0,), work=2,
    )
    x0, x1, x2, x3 = call(
        along_kernel, "along", (z0, z1, z2, z3),
        [((64, 2 * UNITS), F32)] + [((64, 2 * UNITS), BF16)] * 3, placed=True, after=(s1,),
    )
    base, merged = call(
        return_kernel, "return", (mine, r1, r2, r3, inv, adjt, merged),
        [((ROWS, LANES), F32), ((CHIPS, LANES + 2 * SLOTS, LANES), BF16)],
        scratch=[pltpu.VMEM((CHIPS, 2 * SLOTS, LANES), BF16), pltpu.SemaphoreType.DMA],
        loose=(1,), aliases={6: 1}, after=(x0,),
    )
    same_core = [[2 * chip + core for chip in range(CHIPS)] for core in range(2)]
    parts = lax.all_to_all(merged, "nodes", 0, 0, tiled=True, axis_index_groups=same_core)
    block = ((CHIPS, SLOTS, LANES), BF16)
    mine_back, give_back = call(hand_kernel, "hand", (parts,), [block, block], placed=True)
    mate_back = swap(give_back)
    x2, x1, x3 = near([(2, x2), (1, x1), (3, x3)], True)
    grad_w_second, grad_w_first = call(
        lambda *refs: weights_kernel(scale, *refs), "weights", (x0, x1, x2, x3, parts),
        [((64, 2, UNITS), F32), ((SLOTS, 2, UNITS), F32)], after=(give_back,),
    )
    grad_features = call(
        final_kernel, "final", (base, selt, mine_back, mate_back), [((ROWS, LANES), F32)],
        placed=True, scratch=[pltpu.VMEM((CHIPS, 2, SLOTS, LANES), BF16)],
    )
    return grad_w_first, grad_w_second, grad_features


def solution(mesh):
    placed = (
        P("nodes", "hid"),
        P("nodes", None),
        P("nodes"),
        P("nodes", None, None),
        P("nodes"),
        P(None, None, "hid"),
        P(None, "hid", None),
        P("nodes", "hid"),
    )
    return jax.shard_map(
        on_device,
        mesh=mesh,
        in_specs=placed,
        out_specs=(P("nodes", None, "hid"), P("nodes", None, "hid"), P("nodes", "hid")),
        check_vma=False,
    )
```

```python
import math

import jax
import jax.numpy as jnp
from jax import lax
from jax.experimental import pallas as pl
from jax.experimental.pallas import tpu as pltpu
from jax.sharding import PartitionSpec as P

BF16 = jnp.bfloat16
F32 = jnp.float32
ROWS = 256
PEERS = 32
SLOTS = 16
FAR = PEERS * SLOTS
HID = 4
LANES = 128
UNITS = 512
KEPT = 80
CHIPS = 16
BIG = 2 * ROWS * UNITS * UNITS


def mm(left_op, right_op):
    return jnp.dot(left_op, right_op, preferred_element_type=F32)


def mm_last(left_op, right_op):
    return lax.dot_general(left_op, right_op, (((1,), (1,)), ((), ())), preferred_element_type=F32)


def mm_first(left_op, right_op):
    return lax.dot_general(left_op, right_op, (((0,), (0,)), ((), ())), preferred_element_type=F32)


def wide(column, width):
    return jnp.concatenate([column] * (width // LANES), axis=1)


def route_rows(routes_ref):
    peer = lax.broadcasted_iota(jnp.int32, (PEERS, FAR), 0)
    lane_peer = lax.broadcasted_iota(jnp.int32, (PEERS, FAR), 1) >> 4
    spread_out = jnp.where(peer == lane_peer, 1.0, 0.0).astype(BF16)
    by_slot = mm(routes_ref[...].astype(F32).astype(BF16), spread_out)
    slot = lax.broadcasted_iota(jnp.int32, (SLOTS, FAR), 0)
    lane_slot = lax.broadcasted_iota(jnp.int32, (SLOTS, FAR), 1) & (SLOTS - 1)
    routes = jnp.sum(jnp.where(slot == lane_slot, by_slot, 0.0), axis=0, keepdims=True)
    row = lax.broadcasted_iota(jnp.int32, (ROWS, FAR), 0).astype(F32)
    return jnp.where(row == routes, 1.0, 0.0)


def pick_kernel(routes_ref, feat_ref, sel_ref, send_ref):
    row_peer = lax.broadcasted_iota(jnp.int32, (FAR, PEERS), 0) >> 4
    peer = lax.broadcasted_iota(jnp.int32, (FAR, PEERS), 1)
    by_slot = mm_last(jnp.where(row_peer == peer, 1.0, 0.0).astype(BF16), routes_ref[...].astype(F32).astype(BF16))
    row_slot = lax.broadcasted_iota(jnp.int32, (FAR, SLOTS), 0) & (SLOTS - 1)
    slot = lax.broadcasted_iota(jnp.int32, (FAR, SLOTS), 1)
    routes = jnp.sum(jnp.where(row_slot == slot, by_slot, 0.0), axis=1, keepdims=True)
    row = lax.broadcasted_iota(jnp.int32, (FAR, ROWS), 1).astype(F32)
    sel = jnp.where(row == routes, 1.0, 0.0).astype(BF16)
    sel_ref[...] = sel
    picked = mm(sel, feat_ref[...]).astype(BF16).reshape(PEERS, SLOTS, LANES)
    for part in range(HID):
        send_ref[:, part] = picked


def count_kernel(
    neigh_ref, degree_ref, adj_ref, adjt_ref, inv_ref, key_ref, low_ref, high_ref
):
    inv_ref[...] = 1.0 / jnp.broadcast_to(degree_ref[...].astype(F32), (LANES, ROWS)).T
    entry = neigh_ref[...]
    used = lax.broadcasted_iota(jnp.int32, (KEPT, ROWS), 0) < degree_ref[...]
    block = entry >> 7
    upper = block >= 3
    weight = jnp.where(used, jnp.left_shift(1, 10 * jnp.where(upper, block - 3, block)), 0)
    key_ref[...] = entry & (LANES - 1)
    low_ref[...] = jnp.where(upper, 0, weight)
    high_ref[...] = jnp.where(upper, weight, 0)
    tall = 64
    for half in range(LANES // tall):
        value = lax.broadcasted_iota(jnp.int32, (tall, LANES), 0) + half * tall
        for side in range(ROWS // LANES):
            cols = slice(side * LANES, (side + 1) * LANES)

            def step(index, carry):
                low, high = carry
                at = pl.ds(pl.multiple_of(index * 8, 8), 8)
                keys, lows, highs = key_ref[at, cols], low_ref[at, cols], high_ref[at, cols]
                for j in range(8):
                    same = keys[j : j + 1] == value
                    low = low + jnp.where(same, lows[j : j + 1], 0)
                    high = high + jnp.where(same, highs[j : j + 1], 0)
                return low, high

            empty = jnp.zeros((tall, LANES), jnp.int32)
            low, high = lax.fori_loop(0, KEPT // 8, step, (empty, empty))
            for t in range(3):
                for base, packed in ((0, low), (3, high)):
                    count = jnp.right_shift(packed, 10 * t) & 1023
                    start = (base + t) * LANES + half * tall
                    adjt_ref[start : start + tall, cols] = count.astype(F32).astype(BF16)
    for t in range((ROWS + FAR) // LANES):
        rows = slice(t * LANES, (t + 1) * LANES)
        adj_ref[:, rows] = adjt_ref[rows, :].astype(F32).T.astype(BF16)


def first_kernel(
    place, f0, f1, f2, f3, far_ref, adj_ref, inv_ref, w_ref, sel_ref, both_ref, hidden_ref, send_ref, far_all
):
    for d, piece in enumerate((f0, f1, f2, f3)):
        origin = lax.rem(place.hid + HID - d, HID)
        both_ref[:, pl.ds(pl.multiple_of(origin * LANES, LANES), LANES)] = piece[...]
    for origin in range(HID):
        far_all[:, origin * LANES : (origin + 1) * LANES] = far_ref[:, origin].reshape(FAR, LANES)
    agg = mm(adj_ref[:, :ROWS], both_ref[:, :UNITS]) + mm(adj_ref[:, ROWS:], far_all[...])
    both_ref[:, UNITS:] = (agg * wide(inv_ref[...], UNITS)).astype(BF16)
    pre = mm(both_ref[...], w_ref[...])
    sig = 1.0 / (1.0 + jnp.exp(-pre))
    hidden = (pre * sig).astype(BF16)
    hidden_ref[...] = hidden
    send_ref[...] = mm(sel_ref[...], hidden).astype(BF16).reshape(PEERS, SLOTS, UNITS)


def gate_kernel(both_ref, stacked_ref, w1_ref, routes_ref, slope_ref, saved_ref, selt_ref):
    selt_ref[...] = route_rows(routes_ref).astype(BF16)
    saved_ref[...] = stacked_ref[...]
    pre = mm(both_ref[...], w1_ref[...])
    sig = 1.0 / (1.0 + jnp.exp(-pre))
    slope_ref[...] = (sig * (1.0 + pre * (1.0 - sig))).astype(slope_ref.dtype)


def second_kernel(
    place, hidden_ref, far_ref, adj_ref, inv_ref, w_ref, stacked_ref, own_a, own_b, s1a, s1b, s2a, s2b, s3a, s3b
):
    hidden = hidden_ref[...]
    total = mm(adj_ref[:, :ROWS], hidden) + mm(adj_ref[:, ROWS:], far_ref[...].reshape(FAR, UNITS))
    stacked_ref[:, :UNITS] = hidden
    stacked_ref[:, UNITS:] = (total * wide(inv_ref[...], UNITS)).astype(BF16)
    for d, upper, lower in ((2, s2a, s2b), (1, s1a, s1b), (3, s3a, s3b), (0, own_a, own_b)):
        target = lax.rem(place.hid + d, HID)
        cols = pl.ds(pl.multiple_of(target * UNITS, UNITS), UNITS)
        part = mm(stacked_ref[...], w_ref[:, cols]).astype(upper.dtype)
        upper[...] = part[: ROWS // 2]
        lower[...] = part[ROWS // 2 :]


def choose_kernel(place, both_ref, mine_ref, give_ref):
    row = lax.broadcasted_iota(jnp.int32, (UNITS, UNITS // 2), 0)
    col = lax.broadcasted_iota(jnp.int32, (UNITS, UNITS // 2), 1)
    for core, out in ((place.core, mine_ref), (1 - place.core, give_ref)):
        keep = jnp.where(row == (col >> 4) * 32 + core * 16 + (col & 15), 1.0, 0.0).astype(BF16)
        for kind in range(2):
            cols = slice(kind * UNITS, (kind + 1) * UNITS)
            out[:, kind * UNITS // 2 : (kind + 1) * UNITS // 2] = mm(both_ref[:, cols], keep).astype(BF16)


def slope_kernel(first_row, count_ref, own_ref, r1, r2, r3, cot_ref, grad_ref):
    pre = own_ref[...] + r1[...].astype(F32) + r2[...].astype(F32) + r3[...].astype(F32)
    sig = 1.0 / (1.0 + jnp.exp(-pre))
    slope = cot_ref[first_row : first_row + ROWS // 2, :].astype(F32) * (sig * (1.0 + pre * (1.0 - sig)))
    live = lax.broadcasted_iota(jnp.int32, pre.shape, 0) + first_row < count_ref[0]
    grad_ref[...] = jnp.where(live, slope, 0.0).astype(BF16)


def spread_kernel(
    place, g0a, g0b, g1a, g1b, g2a, g2b, g3a, g3b, w_ref, inv_ref, adjt_ref, halo_ref, own_hbm, others_ref,
    own_ref, sems,
):
    parts = ((g0a, g0b), (g1a, g1b), (g2a, g2b), (g3a, g3b))
    rows = ROWS // 2
    copies = [
        pltpu.make_async_copy(ref, others_ref.at[d, pl.ds(half * rows, rows)], sems.at[2 * d + half])
        for d, pair in enumerate(parts)
        for half, ref in enumerate(pair)
    ]
    for copy in copies:
        copy.start()
    grads = {d: jnp.concatenate([upper[...], lower[...]], axis=0) for d, (upper, lower) in enumerate(parts)}

    def back(base):
        total = None
        for d in (0, 3, 1, 2):
            origin = lax.rem(place.hid + HID - d, HID)
            cols = pl.ds(pl.multiple_of(origin * UNITS, UNITS), UNITS)
            term = mm_last(grads[d], w_ref[base : base + UNITS, cols])
            total = term if total is None else total + term
        return total

    mean = (back(UNITS) * wide(inv_ref[...], UNITS)).astype(BF16)
    own_ref[...] = (back(0) + mm(adjt_ref[:ROWS, :], mean)).astype(BF16)
    copies.append(pltpu.make_async_copy(own_ref, own_hbm, sems.at[8]))
    copies[-1].start()
    halo_ref[...] = mm(adjt_ref[ROWS:, :], mean).astype(BF16).reshape(PEERS, SLOTS, UNITS)
    for copy in copies:
        copy.wait()


def outer_second_kernel(slots, place, grads_hbm, mates_ref, stacked_hbm, mate_ref, *refs):
    outs, (block_ref, grads_ref, mine_ref, load_sems, sems) = refs[:4], refs[4:]
    loads = [pltpu.make_async_copy(grads_hbm.at[0], grads_ref.at[0], load_sems.at[0])]
    for source, target, base in ((stacked_hbm, mine_ref, 4),):
        for piece in range(2):
            rows = pl.ds(piece * ROWS // 2, ROWS // 2)
            loads.append(pltpu.make_async_copy(source.at[rows], target.at[rows], load_sems.at[base + piece]))
    loads += [
        pltpu.make_async_copy(grads_hbm.at[index], grads_ref.at[index], load_sems.at[index]) for index in (1, 2, 3)
    ]
    for load in loads:
        load.start()
    row = lax.broadcasted_iota(jnp.int32, (UNITS, UNITS // 2), 0)
    col = lax.broadcasted_iota(jnp.int32, (UNITS, UNITS // 2), 1)
    wanted = (col >> 6) * 128 + place.core * 64 + (col & 63)
    keep = jnp.where(row == wanted, 1.0, 0.0).astype(BF16)
    for index, slot in enumerate(slots):
        other = mm(mates_ref[index], keep).astype(BF16)
        loads[index + 2 if index else 0].wait()
        mine = mm(grads_ref[index], keep).astype(BF16)
        if index == 0:
            for load in loads[1:3]:
                load.wait()
        total = mm_first(mine, mine_ref[...]) + mm_first(other, mate_ref[...])
        block_ref[index] = total.astype(BF16).reshape(HID, 64, 2 * UNITS)

        @pl.when(place.core == 0)
        def _():
            for d, out in enumerate(outs):
                source = block_ref.at[index, lax.rem(place.z + d, HID)]
                pltpu.make_async_copy(source, out.at[slot], sems.at[index, d]).start()

        step = lax.rem(place.hid + 2 * HID - place.x - slot, HID)
        for d, out in enumerate(outs):

            @pl.when((place.core == 1) & (step == d))
            def _():
                for z in range(HID):
                    pltpu.make_async_copy(block_ref.at[index, z], out.at[z], sems.at[index, z]).start()

    for index, slot in enumerate(slots):
        for d, out in enumerate(outs):
            pltpu.make_async_copy(block_ref.at[index, d], out.at[slot], sems.at[index, d]).wait()


def along_kernel(place, z0, z1, z2, z3, x0, x1, x2, x3):
    for d, out in enumerate((x0, x1, x2, x3)):
        by_x = lax.rem(place.hid + 2 * HID - place.x - d, HID)
        at = jnp.where(place.core == 0, by_x, lax.rem(place.z + d, HID))
        total = z0[at].astype(F32) + z1[at].astype(F32) + z2[at].astype(F32) + z3[at].astype(F32)
        out[...] = total.astype(out.dtype)


def settle_kernel(
    place, back_ref, own_ref, slope_ref, selt_ref, w_ref, grad_ref, mine_ref, s1, s2, s3, full_ref
):
    me = place.hid
    grad = own_ref[...].astype(F32) + mm(selt_ref[...], back_ref[...].reshape(FAR, UNITS))
    grad = (grad * slope_ref[...].astype(F32)).astype(BF16)
    grad_ref[...] = grad
    full_ref[...] = mm_last(grad, w_ref[...])
    for d, out in ((2, s2), (1, s1), (3, s3), (0, mine_ref)):
        target = lax.rem(me + d, HID)
        for half, base in ((1, 0), (0, UNITS)):
            cols = pl.ds(pl.multiple_of(base + target * LANES, LANES), LANES)
            out[:, half * LANES : (half + 1) * LANES] = full_ref[:, cols].astype(out.dtype)


def outer_first_kernel(grad_ref, grad_mate_ref, mine_ref, mate_ref, out_ref):
    product = mm_first(mine_ref[...], grad_ref[...]) + mm_first(mate_ref[...], grad_mate_ref[...])
    product = product.astype(BF16).reshape(2, CHIPS, SLOTS, UNITS)
    for part in range(HID):
        for kind in range(2):
            start = (part * 2 + kind) * SLOTS
            out_ref[:, start : start + SLOTS] = product[kind, :, :, part * LANES : (part + 1) * LANES]


def return_kernel(mine_ref, r1, r2, r3, inv_ref, adjt_ref, merged_ref, base_ref, out_ref, halo_ref, sem):
    total = mine_ref[...] + r1[...].astype(F32) + r2[...].astype(F32) + r3[...].astype(F32)
    mean = (total[:, :LANES] * inv_ref[...]).astype(BF16)
    halo_ref[...] = mm(adjt_ref[ROWS:, :], mean).astype(BF16).reshape(CHIPS, 2 * SLOTS, LANES)
    copy = pltpu.make_async_copy(halo_ref, out_ref.at[:, pl.ds(LANES, 2 * SLOTS), :], sem)
    copy.start()
    base_ref[...] = total[:, LANES:] + mm(adjt_ref[:ROWS, :], mean)
    copy.wait()


def hand_kernel(place, parts_ref, mine_ref, give_ref):
    for core, out in ((place.core, mine_ref), (1 - place.core, give_ref)):
        out[...] = parts_ref[:, pl.ds(pl.multiple_of(LANES + core * SLOTS, SLOTS), SLOTS), :]


def weights_kernel(scale, x0, x1, x2, x3, parts_ref, second_ref, first_ref):
    total = parts_ref[0, :LANES].astype(F32)
    for index in range(1, CHIPS):
        total = total + parts_ref[index, :LANES].astype(F32)
    total = total * scale
    for part in range(HID):
        for kind in range(2):
            start = (part * 2 + kind) * SLOTS
            first_ref[:, kind, part * LANES : (part + 1) * LANES] = total[start : start + SLOTS]
    total = (x0[...] + x1[...].astype(F32) + x2[...].astype(F32) + x3[...].astype(F32)) * scale
    second_ref[:, 0, :] = total[:, :UNITS]
    second_ref[:, 1, :] = total[:, UNITS:]


def final_kernel(place, base_ref, selt_ref, mine_ref, mate_ref, feat_ref, back_ref):
    back_ref[:, place.core] = mine_ref[...]
    back_ref[:, 1 - place.core] = mate_ref[...]
    feat_ref[...] = base_ref[...] + mm(selt_ref[...], back_ref[...].reshape(FAR, LANES))


class Place:
    def __init__(self):
        node = lax.axis_index("nodes")
        self.hid = lax.axis_index("hid")
        self.core = node & 1
        self.x = node >> 3
        self.z = (node >> 1) & 3


class Late:
    def __init__(self, source, ref, sem):
        self.ref = ref
        self.source = source
        self.copy = pltpu.make_async_copy(source, ref, sem)
        self.copy.start()
        self.waited = False

    def __getitem__(self, index):
        if not self.waited:
            self.copy.wait()
            self.waited = True
        return self.ref[index]


def in_hbm(value):
    return pltpu.with_memory_space_constraint(value, pltpu.HBM)


def call(
    kernel, name, operands, outs, scratch=(), placed=False, scalars=0, after=(), late=(), held=(), stored=(),
    loose=(), pinned=(), aliases=None, work=1,
):
    shapes = [jax.ShapeDtypeStruct(shape, dtype) for shape, dtype in outs]
    for index in (*stored, *loose):
        shapes[index] = pltpu.HBM(*outs[index])
    for index in pinned:
        shapes[index] = pltpu.VMEM(*outs[index])
    operands = [in_hbm(o) if index in (*late, *held) else o for index, o in enumerate(operands)]
    count = len(operands)
    in_specs = [
        pl.BlockSpec(memory_space=pltpu.SMEM if index < scalars else pltpu.VMEM) for index in range(count)
    ] + [pl.BlockSpec(memory_space=pl.ANY)] * len(after)
    for index in (*late, *held, *(aliases or {})):
        in_specs[index] = pl.BlockSpec(memory_space=pltpu.HBM)
    out_specs = [
        pl.BlockSpec(memory_space=pltpu.HBM if index in (*stored, *loose) else pltpu.VMEM)
        for index in range(len(shapes))
    ]
    first_out = count + len(after)
    fixed = first_out + len(shapes) + len(scratch)
    buffers = [pltpu.VMEM(operands[index].shape, operands[index].dtype) for index in late]
    buffers += [pltpu.VMEM(*outs[index]) for index in stored]
    sems = [pltpu.SemaphoreType.DMA for _ in buffers]

    def body(*refs):
        inputs = list(refs[:count])
        outputs = list(refs[first_out : first_out + len(shapes)])
        spare, flags = refs[fixed : fixed + len(buffers)], refs[fixed + len(buffers) :]
        for slot, index in enumerate(late):
            inputs[index] = Late(inputs[index], spare[slot], flags[slot])
        copies = []
        for slot, index in enumerate(stored, len(late)):
            copies.append(pltpu.make_async_copy(spare[slot], outputs[index], flags[slot]))
            outputs[index] = spare[slot]
        kernel(*([Place()] if placed else []), *inputs, *outputs, *refs[first_out + len(shapes) : fixed])
        for copy in copies:
            copy.start()
        for copy in copies:
            copy.wait()

    moved = sum(o.size * o.dtype.itemsize for o in operands) + sum(
        math.prod(shape) * jnp.dtype(dtype).itemsize for shape, dtype in outs
    )
    results = pl.pallas_call(
        body,
        out_shape=shapes,
        in_specs=in_specs,
        out_specs=out_specs,
        scratch_shapes=list(scratch) + buffers + sems,
        input_output_aliases=aliases or {},
        compiler_params=pltpu.CompilerParams(vmem_limit_bytes=16 * 1024 * 1024),
        cost_estimate=pl.CostEstimate(flops=work * BIG, bytes_accessed=moved, transcendentals=0),
        name=name,
    )(*operands, *after)
    return results[0] if len(outs) == 1 else results


def around(values):
    return [lax.ppermute(v, "hid", [(i, (i + d) % HID) for i in range(HID)]) for d, v in values]


def node_at(x, z, core):
    return ((x % 4) * 4 + z % 4) * 2 + core


def swap(value):
    return lax.ppermute(value, "nodes", [(i, i ^ 1) for i in range(PEERS)])


def near(values, turned):
    def target(x, z, core, d):
        return node_at(x, z + d, core) if (core == 0) != turned else node_at(x + d, z, core)

    return [
        lax.ppermute(v, "nodes", [
            (node_at(x, z, c), target(x, z, c, d)) for x in range(4) for z in range(4) for c in range(2)
        ])
        for d, v in values
    ]


def on_device(features, neighbors, degree, send_rows, node_count, w_first, w_second, cotangent):
    scale = float(ROWS * PEERS) ** (-0.5)
    routes = jnp.swapaxes(send_rows, 1, 2).reshape(SLOTS, PEERS)
    w1 = w_first.reshape(2 * UNITS, UNITS)
    w2 = w_second.reshape(2 * UNITS, HID * UNITS)
    chunk = ((ROWS, UNITS), BF16)

    wide_chunk = ((ROWS, UNITS), F32)
    halo = ((PEERS, SLOTS, UNITS), BF16)
    sel, send_feat = call(
        pick_kernel, "pick", (routes, features),
        [((FAR, ROWS), BF16), ((PEERS, HID, SLOTS, LANES), BF16)], late=(0, 1), work=1,
    )
    far_feat = lax.all_to_all(
        send_feat.reshape(PEERS * HID, SLOTS, LANES), ("nodes", "hid"), 0, 0, tiled=True
    ).reshape(PEERS, HID, SLOTS, LANES)
    f1, f3, f2 = around([(1, features), (3, features), (2, features)])
    adj, adjt, inv = call(
        count_kernel, "count", (jnp.swapaxes(neighbors, 0, 1), degree.reshape(1, ROWS)),
        [((ROWS, ROWS + FAR), BF16), ((ROWS + FAR, ROWS), BF16), ((ROWS, LANES), F32)],
        scratch=[pltpu.VMEM((KEPT, ROWS), jnp.int32)] * 3, late=(1, 0), work=8, after=(sel,),
    )
    both, hidden, send_hidden = call(
        first_kernel, "first", (features, f1, f2, f3, far_feat, adj, inv, w1, sel),
        [((ROWS, 2 * UNITS), BF16), chunk, halo], work=60, placed=True,
        scratch=[pltpu.VMEM((FAR, UNITS), BF16)],
    )
    far_hidden = lax.all_to_all(send_hidden, "nodes", 0, 0, tiled=True)
    half_chunk = ((ROWS // 2, UNITS), BF16)
    stacked, own_a, own_b, s1a, s1b, s2a, s2b, s3a, s3b = call(
        second_kernel, "second", (hidden, far_hidden, adj, inv, w2),
        [((ROWS, 2 * UNITS), BF16)] + [((ROWS // 2, UNITS), F32)] * 2 + [half_chunk] * 6,
        placed=True, work=10,
    )
    r1a, r3a, r2a = around([(1, s1a), (3, s3a), (2, s2a)])
    r1b, r3b, r2b = around([(1, s1b), (3, s3b), (2, s2b)])
    slope, saved, selt = call(
        gate_kernel, "gate", (both, stacked, w1, routes),
        [chunk, ((ROWS, 2 * UNITS), BF16), ((ROWS, FAR), BF16)],
        after=(s1a,), late=(3,), stored=(0, 1, 2), work=2,
    )
    saved_mate = swap(saved)
    def gradient(first_row, own, parts):
        return call(
            lambda *refs: slope_kernel(first_row, *refs), "slope", (node_count, own, *parts, cotangent),
            [half_chunk], scalars=1, after=(in_hbm(slope),),
        )

    g0a = gradient(0, own_a, (r1a, r2a, r3a))
    g1a, g3a, g2a = around([(1, g0a), (3, g0a), (2, g0a)])
    g0b = gradient(ROWS // 2, own_b, (r1b, r2b, r3b))
    g1b, g3b, g2b = around([(1, g0b), (3, g0b), (2, g0b)])

    mine_rows, give_rows = call(
        choose_kernel, "choose", (both,), [chunk, chunk], placed=True, stored=(0, 1), work=4, after=(g0b,),
    )
    mate_rows = swap(give_rows)
    halo_hidden, own_hidden, others = call(
        spread_kernel, "spread", (g0a, g0b, g1a, g1b, g2a, g2b, g3a, g3b, w2, inv, adjt),
        [halo, chunk, ((HID, ROWS, UNITS), BF16)], placed=True, work=10, loose=(1, 2), after=(in_hbm(mine_rows),),
        scratch=[pltpu.VMEM((ROWS, UNITS), BF16), pltpu.SemaphoreType.DMA((9,))],
    )
    back_hidden = lax.all_to_all(halo_hidden, "nodes", 0, 0, tiled=True)
    slots = (0, 1, 2, 3)
    z0, z1, z2, z3 = call(
        lambda *refs: outer_second_kernel(slots, *refs), "outer_second",
        (others, swap(others), saved, saved_mate), [((HID, 64, 2 * UNITS), BF16)] * HID,
        scratch=[
            pltpu.VMEM((HID, HID, 64, 2 * UNITS), BF16), pltpu.VMEM((HID, ROWS, UNITS), BF16),
            pltpu.VMEM((ROWS, 2 * UNITS), BF16), pltpu.SemaphoreType.DMA((8,)),
            pltpu.SemaphoreType.DMA((HID, HID)),
        ],
        placed=True, loose=slots, held=(0, 2), work=12,
    )
    outer_done = in_hbm(z0)
    z2, z1, z3 = near([(2, z2), (1, z1), (3, z3)], False)
    grad, mine, s1, s2, s3 = call(
        settle_kernel, "settle",
        (back_hidden, own_hidden, slope, selt, w1),
        [chunk, ((ROWS, 2 * LANES), F32)] + [((ROWS, 2 * LANES), BF16)] * 3,
        scratch=[pltpu.VMEM((ROWS, 2 * UNITS), F32)], placed=True, late=(3, 1, 2, 4), work=40, after=(outer_done,),
    )
    r1, r3, r2 = around([(1, s1), (3, s3), (2, s2)])
    merged = call(
        outer_first_kernel, "outer_first", (grad, swap(grad), mine_rows, mate_rows),
        [((CHIPS, LANES + 2 * SLOTS, LANES), BF16)], after=(s1,), late=(2,), stored=(0,), work=2,
    )
    x0, x1, x2, x3 = call(
        along_kernel, "along", (z0, z1, z2, z3),
        [((64, 2 * UNITS), F32)] + [((64, 2 * UNITS), BF16)] * 3, placed=True, after=(s1,),
    )
    base, merged = call(
        return_kernel, "return", (mine, r1, r2, r3, inv, adjt, merged),
        [((ROWS, LANES), F32), ((CHIPS, LANES + 2 * SLOTS, LANES), BF16)],
        scratch=[pltpu.VMEM((CHIPS, 2 * SLOTS, LANES), BF16), pltpu.SemaphoreType.DMA],
        loose=(1,), aliases={6: 1}, after=(x0,),
    )
    same_core = [[2 * chip + core for chip in range(CHIPS)] for core in range(2)]
    parts = lax.all_to_all(merged, "nodes", 0, 0, tiled=True, axis_index_groups=same_core)
    block = ((CHIPS, SLOTS, LANES), BF16)
    mine_back, give_back = call(hand_kernel, "hand", (parts,), [block, block], placed=True)
    mate_back = swap(give_back)
    x2, x1, x3 = near([(2, x2), (1, x1), (3, x3)], True)
    grad_w_second, grad_w_first = call(
        lambda *refs: weights_kernel(scale, *refs), "weights", (x0, x1, x2, x3, parts),
        [((64, 2, UNITS), F32), ((SLOTS, 2, UNITS), F32)], after=(give_back,),
    )
    grad_features = call(
        final_kernel, "final", (base, selt, mine_back, mate_back), [((ROWS, LANES), F32)],
        placed=True, scratch=[pltpu.VMEM((CHIPS, 2, SLOTS, LANES), BF16)],
    )
    return grad_w_first, grad_w_second, grad_features


def solution(mesh):
    placed = (
        P("nodes", "hid"),
        P("nodes", None),
        P("nodes"),
        P("nodes", None, None),
        P("nodes"),
        P(None, None, "hid"),
        P(None, "hid", None),
        P("nodes", "hid"),
    )
    return jax.shard_map(
        on_device,
        mesh=mesh,
        in_specs=placed,
        out_specs=(P("nodes", None, "hid"), P("nodes", None, "hid"), P("nodes", "hid")),
        check_vma=False,
    )
```
